128 devices in a mesh: ctx: 4 (over y_hi, core), seq: 32 (over y_lo, z, x).
Axes of the slice: x: 4, y: 4 (y_hi: 2, y_lo: 2; y = y_hi * 2 + y_lo), z: 4, core: 2. Of those that a mesh axis runs over, the one named last changes fastest.
Arguments:
- bottom_codes: int32 [4, 32768], P(None, ('ctx', 'seq')), may hold values from 0 to 2047
- cond_codes: int32 [4, 8192], P(None, ('ctx', 'seq')), may hold values from 0 to 2047
- bottom_table: bfloat16 [2048, 1024], replicated, may hold values from -4.1875 to 4.1875
- cond_table: bfloat16 [2048, 1024], replicated, may hold values from -4.1875 to 4.1875
- conv_dilated: bfloat16 [3, 1024, 1024], replicated, may hold values from -0.109375 to 0.109375
- conv_mix: bfloat16 [1024, 1024], replicated, may hold values from -0.1875 to 0.1875
- projection: bfloat16 [1024, 1920], replicated, may hold values from -0.1875 to 0.1875
- norm_gain: float32 [1920], replicated, may hold values from 0.5 to 1.5
- norm_bias: float32 [1920], replicated, may hold values from -3 to 3
- attn_weight: bfloat16 [1920, 1440], replicated
Outputs:
- attended: bfloat16 [4, 32768, 480], P(None, ('ctx', 'seq'))
The draws below stay inside these ranges and needn't reach their ends.
All inputs are finite; a program needn't handle non-finite values.
Results may differ from the reference program's by a relative error of at most 0.0065.
Values may be sent and summed in bfloat16 or wider, within the bound.
A program may use at most 128 MiB of HBM per device.

```python
import math
import jax
import jax.numpy as jnp
from jax import lax

D_CONV = 1024
WIDTH = 1920
ATTN = 480
VOCAB = 2048
BLOCK = 128
CONTEXT = 8192
DILATION = 2187
UPSAMPLE = 4
SONGS = 4
TOKENS = 32768
COND = 8192
N_CTX = 4


def draw_attn_weight(key, part):
    base = jax.random.normal(jax.random.fold_in(key, 11), (WIDTH, 3 * ATTN), jnp.float32) / math.sqrt(WIDTH)
    return base.astype(jnp.bfloat16)


def set_ends(values, rng, smallest, high):
    spot = [jax.random.randint(jax.random.fold_in(rng, axis), (), 0, length) for axis, length in enumerate(values.shape)]
    main_axis = values.shape.index(max(values.shape))
    next_to = spot[:main_axis] + [(spot[main_axis] + 1) % values.shape[main_axis]] + spot[main_axis + 1:]
    return values.at[tuple(spot)].set(smallest).at[tuple(next_to)].set(high)


def centred(key, extent, width, bound, dtype=jnp.bfloat16):
    values = jax.random.normal(key, extent, jnp.float32) * width
    return jnp.minimum(jnp.maximum(values, -bound), bound).astype(dtype)


def setup_inputs(seed: int = 0) -> dict:
    arg_keys = jax.random.split(jax.random.key(seed), 11)
    bottom_codes = set_ends(jax.random.randint(arg_keys[0], (SONGS, TOKENS), 0, VOCAB), jax.random.fold_in(arg_keys[0], 1), 0, VOCAB - 1).astype(jnp.int32)
    cond_codes = set_ends(jax.random.randint(arg_keys[1], (SONGS, COND), 0, VOCAB), jax.random.fold_in(arg_keys[1], 1), 0, VOCAB - 1).astype(jnp.int32)
    bottom_table = centred(arg_keys[2], (VOCAB, D_CONV), 0.7, 4.1875)
    cond_table = centred(arg_keys[3], (VOCAB, D_CONV), 0.7, 4.1875)
    conv_dilated = centred(arg_keys[4], (3, D_CONV, D_CONV), (3 * D_CONV) ** -0.5, 0.109375)
    conv_mix = centred(arg_keys[5], (D_CONV, D_CONV), D_CONV ** -0.5, 0.1875)
    projection = centred(arg_keys[6], (D_CONV, WIDTH), D_CONV ** -0.5, 0.1875)
    norm_gain = jnp.clip(1.0 + 0.1 * jax.random.normal(arg_keys[7], (WIDTH,), jnp.float32), 0.5, 1.5)
    norm_bias = centred(arg_keys[8], (WIDTH,), 0.5, 3.0, jnp.float32)
    attn_weight = draw_attn_weight(jax.random.fold_in(arg_keys[10], 71), 0)
    return {"bottom_codes": bottom_codes, "cond_codes": cond_codes, "bottom_table": bottom_table, "cond_table": cond_table, "conv_dilated": conv_dilated, "conv_mix": conv_mix, "projection": projection, "norm_gain": norm_gain, "norm_bias": norm_bias, "attn_weight": attn_weight}


def column_attention(block):
    head = block.shape[-1] // 3
    query = block[..., :head].astype(jnp.float32)
    keys = block[..., head:2 * head].astype(jnp.float32)
    values = block[..., 2 * head:].astype(jnp.float32)
    scores = jnp.einsum('ncd,mcd->cnm', query, keys) * (1.0 / math.sqrt(head))
    count = block.shape[0]
    allowed = jnp.arange(count)[:, None] >= jnp.arange(count)[None, :]
    scores = jnp.where(allowed[None, :, :], scores, -jnp.inf)
    weights = jax.nn.softmax(scores, axis=-1).astype(jnp.bfloat16)
    result = jnp.einsum('cnm,mcd->ncd', weights.astype(jnp.float32), values)
    return result.astype(jnp.bfloat16)

def one_song(codes, cond, bottom_table, cond_table, conv_dilated, conv_mix, projection, norm_gain, norm_bias, attn_weight):
    cond_full = jnp.repeat(cond, UPSAMPLE)
    stream = bottom_table[codes].astype(jnp.float32) + cond_table[cond_full].astype(jnp.float32)
    active = jnp.maximum(stream, 0.0).astype(jnp.bfloat16)
    margin = jnp.zeros((DILATION, active.shape[1]), jnp.bfloat16)
    padded = jnp.concatenate([margin, active, margin], axis=0)
    left = padded[:TOKENS]
    right = padded[2 * DILATION:]
    dilated = jnp.dot(left, conv_dilated[0], preferred_element_type=jnp.float32)
    dilated = dilated + jnp.dot(active, conv_dilated[1], preferred_element_type=jnp.float32)
    dilated = dilated + jnp.dot(right, conv_dilated[2], preferred_element_type=jnp.float32)
    hidden = jnp.maximum(dilated, 0.0).astype(jnp.bfloat16)
    residual = (stream + jnp.dot(hidden, conv_mix, preferred_element_type=jnp.float32)).astype(jnp.bfloat16)
    projected = jnp.dot(residual, projection, preferred_element_type=jnp.float32)
    center = lax.optimization_barrier(jnp.mean(projected, axis=-1, keepdims=True))
    spread = lax.optimization_barrier(jnp.mean((projected - center) ** 2, axis=-1, keepdims=True))
    normed = ((projected - center) / jnp.sqrt(spread + 1e-05) * norm_gain + norm_bias).astype(jnp.bfloat16)
    qkv = jnp.dot(normed, attn_weight, preferred_element_type=jnp.float32).astype(jnp.bfloat16)
    blocks = qkv.reshape(N_CTX, CONTEXT // BLOCK, BLOCK, qkv.shape[-1])
    attended = lax.map(column_attention, blocks)
    return attended.reshape(TOKENS, attended.shape[-1])

def reference(bottom_codes, cond_codes, bottom_table, cond_table, conv_dilated, conv_mix, projection, norm_gain, norm_bias, attn_weight):

    def per_song(pair):
        return one_song(pair[0], pair[1], bottom_table, cond_table, conv_dilated, conv_mix, projection, norm_gain, norm_bias, attn_weight)
    return lax.map(per_song, (bottom_codes, cond_codes))
```

```python
import functools
import math

import jax
import jax.numpy as jnp
from jax import lax
from jax.experimental import pallas as pl
from jax.experimental.pallas import tpu as pltpu
from jax.sharding import PartitionSpec as P

F32, BF16, I32 = jnp.float32, jnp.bfloat16, jnp.int32
MESH = pl.DeviceIdType.MESH

BLOCK = 128
DIL_BLOCKS, DIL_REST = divmod(2187, BLOCK)
CTX, SEQ = 4, 32
ROWS = 256
HALO = 9
SLOTS = SEQ + 2 * HALO
BLOCKS = 64
COLS = 8
CHUNK = BLOCKS * COLS
VOCAB, CH, WIDTH, ATTN = 2048, 1024, 1920, 480
GROUPS = CH // 128
NOWHERE = VOCAB * 8
STAGE = 512
OWN, LEFT, RIGHT = 0, 8, 16
COND = 32
TAPS = (
    (LEFT, (0, 0, 0, 1, 1, 1, 1, 2)),
    (OWN, (0, 0, 0, 0, 1, 1, 1, 1)),
    (RIGHT, (0, 1, 1, 1, 1, 2, 2, 2)),
)


def kernel(
    bottom_ref, cond_ref, gain_ref, bias_ref, btab, ctab, conv, mix, proj, attn,
    out_ref,
    tb, tc, stage, wconv, wmix, wproj, wattn,
    sendc, codes, gath, gsm,
    act, lhs, hidden, resid, pj, normed, qkv, att, sendo,
    stage_sem, w_sem, csend_sem, crecv_sem, g_sem, osend_sem, orecv_sem, local_sem,
):
    a = lax.axis_index("ctx")
    j = lax.axis_index("seq")
    k = j // 2
    h = j % 2

    to_next = jnp.logical_and(a < CTX - 1, j >= SEQ - HALO)
    to_prev = jnp.logical_and(a > 0, j < HALO)

    barrier = pltpu.get_barrier_semaphore()

    def greet(t, _):
        pl.semaphore_signal(
            barrier, inc=1, device_id=(a, lax.rem(j + t, SEQ)), device_id_type=MESH
        )
        return 0

    lax.fori_loop(1, SEQ, greet, 0)

    @pl.when(a > 0)
    def _():
        def f(t, _):
            pl.semaphore_signal(barrier, inc=1, device_id=(a - 1, t), device_id_type=MESH)
            return 0

        lax.fori_loop(SEQ - HALO, SEQ, f, 0)

    @pl.when(a < CTX - 1)
    def _():
        def f(t, _):
            pl.semaphore_signal(barrier, inc=1, device_id=(a + 1, t), device_id_type=MESH)
            return 0

        lax.fori_loop(0, HALO, f, 0)

    def stage_copy(i):
        table = (btab, ctab)[i // 4]
        return pltpu.make_async_copy(
            table.at[pl.ds((i % 4) * STAGE, STAGE)], stage.at[i % 4], stage_sem.at[i % 4]
        )

    weights = [
        pltpu.make_async_copy(src, dst, w_sem.at[i])
        for i, (src, dst) in enumerate(
            ((conv, wconv), (mix, wmix), (proj, wproj), (attn, wattn))
        )
    ]
    for i in range(4):
        stage_copy(i).start()

    sendc[...] = jnp.zeros_like(sendc)
    for song in range(4):
        p, s = divmod(song, 2)
        for u in range(2):
            sendc[p, 2 * s + u : 2 * s + u + 1, :] = bottom_ref[
                song : song + 1, u * 128 : (u + 1) * 128
            ]
            sendc[p, 4 + s : 5 + s, u * 64 : (u + 1) * 64] = cond_ref[song : song + 1, :]

    def widen(i):
        table = (tb, tc)[i // 4]
        stage_copy(i).wait()

        def f(r, _):
            x = stage[i % 4, pl.ds(r * 16, 16), :].astype(F32)
            base = ((i % 4) * STAGE + r * 16) * 8
            for q in range(2):
                for g in range(GROUPS):
                    table[pl.ds(base + q * 64 + g, 8, stride=8), :] = x[
                        8 * q : 8 * q + 8, 128 * g : 128 * g + 128
                    ]
            return 0

        lax.fori_loop(0, STAGE // 16, f, 0, unroll=2)
        if i + 4 < 8:
            stage_copy(i + 4).start()

    for i in range(4):
        widen(i)
    for w in weights:
        w.start()
    tb[pl.ds(NOWHERE, 8), :] = jnp.full((8, 128), -1e9, F32)

    pl.semaphore_wait(barrier, SEQ - 1 + jnp.where(jnp.logical_or(to_next, to_prev), SEQ, 0))

    def send_codes(ctx, peer, slot, sem):
        pltpu.make_async_remote_copy(
            src_ref=sendc.at[peer % 2],
            dst_ref=codes.at[slot],
            send_sem=csend_sem,
            recv_sem=crecv_sem.at[sem],
            device_id=(ctx, peer),
            device_id_type=MESH,
        ).start()

    def own_codes(t, _):
        send_codes(a, lax.rem(j + t, SEQ), j + HALO, 0)
        return 0

    lax.fori_loop(1, SEQ, own_codes, 0)

    @pl.when(to_next)
    def _():
        def f(t, _):
            send_codes(a + 1, t, j - (SEQ - HALO), 1)
            return 0

        lax.fori_loop(0, SEQ, f, 0)

    @pl.when(to_prev)
    def _():
        def f(t, _):
            send_codes(a - 1, t, j + SEQ + HALO, 2)
            return 0

        lax.fori_loop(0, SEQ, f, 0)

    codes[j + HALO] = sendc[h]
    outside = jnp.where(lax.broadcasted_iota(I32, (HALO, 8, 128), 1) < 4, VOCAB, 0)

    @pl.when(a == 0)
    def _():
        codes[0:HALO] = outside

    @pl.when(a == CTX - 1)
    def _():
        codes[SEQ + HALO : SLOTS] = outside

    for i in range(4, 8):
        widen(i)

    def code_wait(count, sem):
        view = codes.at[pl.ds(0, count)]
        pltpu.make_async_copy(view, view, sem).wait()

    code_wait(SEQ - 1, crecv_sem.at[0])

    @pl.when(a > 0)
    def _():
        code_wait(HALO, crecv_sem.at[1])

    @pl.when(a < CTX - 1)
    def _():
        code_wait(HALO, crecv_sem.at[2])

    lanes = lax.broadcasted_iota(I32, (BLOCKS // 2, 128), 1)
    for s in range(2):
        for v in range(2):
            def bottom(beta):
                d, u = divmod(beta, 2)
                return codes[d : d + BLOCKS // 2, 2 * s + u, :]

            def upper(beta):
                d, u = divmod(beta, 2)
                x = codes[d : d + BLOCKS // 2, 4 + s, :]
                if u:
                    y = codes[d + 1 : d + 1 + BLOCKS // 2, 4 + s, :]
                    x = jnp.where(lanes < 64, x, y)
                return x, 32 * u

            lead = v + 2 * HALO
            before, after = lead - DIL_BLOCKS, lead + DIL_BLOCKS
            left = jnp.where(lanes >= 128 - DIL_REST, bottom(before - 1), bottom(before))
            right = jnp.where(lanes < DIL_REST, bottom(after + 1), bottom(after))
            up_own, own0 = upper(lead)
            up_left, left0 = upper(before - 1)
            up_right, right0 = upper(after)
            row = None
            for x, lane0, first, step in (
                (bottom(lead), OWN, 0, COLS),
                (left, LEFT, -DIL_REST, COLS),
                (right, RIGHT, DIL_REST, COLS),
                (up_own, COND + OWN, own0, 2),
                (up_left, COND + LEFT, left0 + 32 - 3, 2),
                (up_right, COND + RIGHT, right0 + 2, 2),
            ):
                amount = lax.rem(lane0 - first + 256 - step * k, 128)
                rolled = pltpu.roll(x, amount, 1)
                row = rolled if row is None else jnp.where(lanes >= lane0, rolled, row)
            gath[pl.ds(s * BLOCKS + v, BLOCKS // 2, stride=2), :] = row
    to_smem = pltpu.make_async_copy(gath, gsm, g_sem)
    to_smem.start()
    to_smem.wait()

    for w in weights:
        w.wait()

    scale = 1.0 / math.sqrt(ATTN)
    half = CHUNK // 2
    ri = lax.broadcasted_iota(I32, (half, half), 0)
    ci = lax.broadcasted_iota(I32, (half, half), 1)
    allowed = jnp.logical_and(ri // BLOCKS == ci // BLOCKS, ci <= ri)

    for s in range(2):
        def gather(b, _):
            r = s * BLOCKS + b
            for t, (lane0, conds) in enumerate(TAPS):
                upper = {
                    c: tc[pl.ds(gsm[r, COND + lane0 + c] * 8, 8), :]
                    for c in sorted(set(conds))
                }
                for c in range(COLS):
                    x = tb[pl.ds(gsm[r, lane0 + c] * 8, 8), :] + upper[conds[c]]
                    act[t, pl.ds(c * BLOCKS + b, 8, stride=CHUNK), :] = x
            return 0

        lax.fori_loop(0, BLOCKS, gather, 0, unroll=2)

        def pack(i, _):
            for t in range(3):
                for g in range(GROUPS):
                    x = act[t, pl.ds(g * CHUNK + i * 64, 64), :]
                    lhs[pl.ds(i * 64, 64), t * CH + g * 128 : t * CH + (g + 1) * 128] = (
                        jnp.maximum(x, 0.0).astype(BF16)
                    )
            return 0

        lax.fori_loop(0, CHUNK // 64, pack, 0)

        for n in range(CH // 512):
            acc = jnp.dot(
                lhs[...], wconv[:, n * 512 : (n + 1) * 512], preferred_element_type=F32
            )
            hidden[:, n * 512 : (n + 1) * 512] = jnp.maximum(acc, 0.0).astype(BF16)

        for n in range(CH // 512):
            acc = jnp.dot(
                hidden[...], wmix[:, n * 512 : (n + 1) * 512], preferred_element_type=F32
            )
            for g in range(4):
                stream = act[1, pl.ds((4 * n + g) * CHUNK, CHUNK), :]
                resid[:, n * 512 + g * 128 : n * 512 + (g + 1) * 128] = (
                    stream + acc[:, g * 128 : (g + 1) * 128]
                ).astype(BF16)

        for n0, n1 in ((0, 512), (512, 1024), (1024, 1536), (1536, WIDTH)):
            pj[:, n0:n1] = jnp.dot(resid[...], wproj[:, n0:n1], preferred_element_type=F32)

        def norm(i, _):
            x = pj[pl.ds(i * 64, 64), :]
            x = x - jnp.mean(x, axis=-1, keepdims=True)
            var = jnp.mean(x * x, axis=-1, keepdims=True)
            y = x / jnp.sqrt(var + 1e-05) * gain_ref[...] + bias_ref[...]
            normed[pl.ds(i * 64, 64), :] = y.astype(BF16)
            return 0

        lax.fori_loop(0, CHUNK // 64, norm, 0)

        for n in range(3):
            qkv[n] = lax.dot_general(
                normed[...],
                wattn[n * ATTN : (n + 1) * ATTN, :],
                (((1,), (1,)), ((), ())),
                preferred_element_type=F32,
            ).astype(BF16)

        for p in range(2):
            rows = slice(p * half, (p + 1) * half)
            query = qkv[0, rows, :]
            keys = qkv[1, rows, :]
            values = qkv[2, rows, :]
            scores = lax.dot_general(
                query, keys, (((1,), (1,)), ((), ())), preferred_element_type=F32
            ) * scale
            scores = jnp.where(allowed, scores, -jnp.inf)
            e = jnp.exp(scores - jnp.max(scores, axis=-1, keepdims=True))
            w = (e / jnp.sum(e, axis=-1, keepdims=True)).astype(BF16)
            mixed = jnp.dot(w, values, preferred_element_type=F32)
            for g in range(4):
                wide = min(128, ATTN - g * 128)
                att[g, rows, 0:wide] = mixed[:, g * 128 : g * 128 + wide]

        def regroup(i, _):
            for v in range(2):
                for g in range(4):
                    x = att[g, pl.ds(2 * i + v, COLS, stride=BLOCKS), :]
                    wide = min(128, ATTN - g * 128)
                    sendo[s, i, v * COLS : (v + 1) * COLS, g * 128 : g * 128 + wide] = x[
                        :, :wide
                    ].astype(BF16)
            return 0

        lax.fori_loop(0, SEQ, regroup, 0, unroll=2)

        song = 2 * h + s

        def send_out(t, _):
            peer = lax.rem(j + t, SEQ)
            pltpu.make_async_remote_copy(
                src_ref=sendo.at[s, peer],
                dst_ref=out_ref.at[song, k],
                send_sem=osend_sem.at[s],
                recv_sem=orecv_sem.at[s],
                device_id=(a, peer),
                device_id_type=MESH,
            ).start()
            return 0

        lax.fori_loop(1, SEQ, send_out, 0)
        pltpu.make_async_copy(sendo.at[s, j], out_ref.at[song, k], local_sem.at[s]).start()

    for s in range(2):
        view = sendo.at[s, pl.ds(0, SEQ - 1)]
        pltpu.make_async_copy(view, view, osend_sem.at[s]).wait()
        pltpu.make_async_copy(view, view, orecv_sem.at[s]).wait()
        pltpu.make_async_copy(sendo.at[s, j], out_ref.at[2 * h + s, k], local_sem.at[s]).wait()
    code_wait(SEQ - 1, csend_sem)

    @pl.when(jnp.logical_or(to_next, to_prev))
    def _():
        code_wait(SEQ, csend_sem)


def body(
    bottom_codes, cond_codes, bottom_table, cond_table, conv_dilated, conv_mix,
    projection, norm_gain, norm_bias, attn_weight,
):
    vmem = pl.BlockSpec(memory_space=pltpu.VMEM)
    hbm = pl.BlockSpec(memory_space=pl.ANY)
    dma = pltpu.SemaphoreType.DMA
    out = pl.pallas_call(
        kernel,
        out_shape=jax.ShapeDtypeStruct((4, SEQ // 2, 16, ATTN), BF16),
        in_specs=[vmem] * 4 + [hbm] * 6,
        out_specs=hbm,
        scratch_shapes=[
            pltpu.VMEM((VOCAB * 8 + 8, 128), F32),
            pltpu.VMEM((VOCAB * 8, 128), F32),
            pltpu.VMEM((4, STAGE, CH), BF16),
            pltpu.VMEM((3 * CH, CH), BF16),
            pltpu.VMEM((CH, CH), BF16),
            pltpu.VMEM((CH, WIDTH), BF16),
            pltpu.VMEM((3 * ATTN, WIDTH), BF16),
            pltpu.VMEM((2, 8, 128), I32),
            pltpu.VMEM((SLOTS, 8, 128), I32),
            pltpu.VMEM((2 * BLOCKS, 128), I32),
            pltpu.SMEM((2 * BLOCKS, 128), I32),
            pltpu.VMEM((3, GROUPS * CHUNK, 128), F32),
            pltpu.VMEM((CHUNK, 3 * CH), BF16),
            pltpu.VMEM((CHUNK, CH), BF16),
            pltpu.VMEM((CHUNK, CH), BF16),
            pltpu.VMEM((CHUNK, WIDTH), F32),
            pltpu.VMEM((CHUNK, WIDTH), BF16),
            pltpu.VMEM((3, CHUNK, ATTN), BF16),
            pltpu.VMEM((4, CHUNK, 128), F32),
            pltpu.VMEM((2, SEQ, 16, ATTN), BF16),
            dma((4,)),
            dma((4,)),
            dma,
            dma((3,)),
            dma,
            dma((2,)),
            dma((2,)),
            dma((2,)),
        ],
        compiler_params=pltpu.CompilerParams(
            collective_id=0, has_side_effects=True, vmem_limit_bytes=63 * 1024 * 1024
        ),
        cost_estimate=pl.CostEstimate(
            flops=18_300_000_000, bytes_accessed=28_000_000, transcendentals=300_000
        ),
        name="upsampler",
    )(
        bottom_codes, cond_codes, norm_gain.reshape(1, WIDTH), norm_bias.reshape(1, WIDTH),
        bottom_table, cond_table, conv_dilated.reshape(3 * CH, CH), conv_mix, projection,
        attn_weight.T,
    )
    songs = bottom_codes.shape[0]
    out = out.reshape(songs, SEQ // 2, 2, COLS, ATTN).transpose(0, 2, 1, 3, 4)
    return out.reshape(songs, ROWS, ATTN)


def solution(mesh):
    split = P(None, ("ctx", "seq"))
    return jax.shard_map(
        body,
        mesh=mesh,
        in_specs=(split, split) + (P(),) * 8,
        out_specs=P(None, ("ctx", "seq"), None),
        check_vma=False,
    )
```

```python
import functools
import math

import jax
import jax.numpy as jnp
from jax import lax
from jax.experimental import pallas as pl
from jax.experimental.pallas import tpu as pltpu
from jax.sharding import PartitionSpec as P

F32, BF16, I32 = jnp.float32, jnp.bfloat16, jnp.int32
MESH = pl.DeviceIdType.MESH

BLOCK = 128
DIL_BLOCKS, DIL_REST = divmod(2187, BLOCK)
CTX, SEQ = 4, 32
ROWS = 256
HALO = 9
SLOTS = SEQ + 2 * HALO
BLOCKS = 64
COLS = 8
CHUNK = BLOCKS * COLS
VOCAB, CH, WIDTH, ATTN = 2048, 1024, 1920, 480
GROUPS = CH // 128
PITCH = CHUNK + 8
CPITCH = BLOCKS + 8
NOWHERE = VOCAB * 8
STAGE = 512
OWN, LEFT, RIGHT = 0, 8, 16
COND = 32
TAPS = (
    (LEFT, (0, 0, 0, 1, 1, 1, 1, 2)),
    (OWN, (0, 0, 0, 0, 1, 1, 1, 1)),
    (RIGHT, (0, 1, 1, 1, 1, 2, 2, 2)),
)


def kernel(
    bottom_ref, cond_ref, gain_ref, bias_ref, btab, ctab, conv, mix, proj, attn,
    out_ref,
    tb, tc, stage, wconv, wmix, wproj, wattn,
    sendc, codes, gath, gsm,
    act, lhs, hidden, resid, pj, normed, qkv, att, sendo,
    stage_sem, w_sem, csend_sem, crecv_sem, g_sem, osend_sem, orecv_sem, local_sem,
):
    a = lax.axis_index("ctx")
    j = lax.axis_index("seq")
    k = j // 2
    h = j % 2

    to_next = jnp.logical_and(a < CTX - 1, j >= SEQ - HALO)
    to_prev = jnp.logical_and(a > 0, j < HALO)

    barrier = pltpu.get_barrier_semaphore()

    def greet(t, _):
        pl.semaphore_signal(
            barrier, inc=1, device_id=(a, lax.rem(j + t, SEQ)), device_id_type=MESH
        )
        return 0

    lax.fori_loop(1, SEQ, greet, 0)

    @pl.when(a > 0)
    def _():
        def f(t, _):
            pl.semaphore_signal(barrier, inc=1, device_id=(a - 1, t), device_id_type=MESH)
            return 0

        lax.fori_loop(SEQ - HALO, SEQ, f, 0)

    @pl.when(a < CTX - 1)
    def _():
        def f(t, _):
            pl.semaphore_signal(barrier, inc=1, device_id=(a + 1, t), device_id_type=MESH)
            return 0

        lax.fori_loop(0, HALO, f, 0)

    def stage_copy(i):
        table = (btab, ctab)[i // 4]
        return pltpu.make_async_copy(
            table.at[pl.ds((i % 4) * STAGE, STAGE)], stage.at[i % 4], stage_sem.at[i % 4]
        )

    weights = [
        pltpu.make_async_copy(src, dst, w_sem.at[i])
        for i, (src, dst) in enumerate(
            ((conv, wconv), (mix, wmix), (proj, wproj), (attn, wattn))
        )
    ]
    for i in range(4):
        stage_copy(i).start()

    sendc[...] = jnp.zeros_like(sendc)
    for song in range(4):
        p, s = divmod(song, 2)
        for u in range(2):
            sendc[p, 2 * s + u : 2 * s + u + 1, :] = bottom_ref[
                song : song + 1, u * 128 : (u + 1) * 128
            ]
            sendc[p, 4 + s : 5 + s, u * 64 : (u + 1) * 64] = cond_ref[song : song + 1, :]

    def widen(i):
        table = (tb, tc)[i // 4]
        stage_copy(i).wait()

        def f(r, _):
            x = stage[i % 4, pl.ds(r * 16, 16), :].astype(F32)
            base = ((i % 4) * STAGE + r * 16) * 8
            for q in range(2):
                for g in range(GROUPS):
                    table[pl.ds(base + q * 64 + g, 8, stride=8), :] = x[
                        8 * q : 8 * q + 8, 128 * g : 128 * g + 128
                    ]
            return 0

        lax.fori_loop(0, STAGE // 16, f, 0, unroll=2)
        if i + 4 < 8:
            stage_copy(i + 4).start()

    for i in range(4):
        widen(i)
    for w in weights:
        w.start()
    tb[pl.ds(NOWHERE, 8), :] = jnp.full((8, 128), -1e9, F32)

    pl.semaphore_wait(barrier, SEQ - 1 + jnp.where(jnp.logical_or(to_next, to_prev), SEQ, 0))

    def send_codes(ctx, peer, slot, sem):
        pltpu.make_async_remote_copy(
            src_ref=sendc.at[peer % 2],
            dst_ref=codes.at[slot],
            send_sem=csend_sem,
            recv_sem=crecv_sem.at[sem],
            device_id=(ctx, peer),
            device_id_type=MESH,
        ).start()

    def own_codes(t, _):
        send_codes(a, lax.rem(j + t, SEQ), j + HALO, 0)
        return 0

    lax.fori_loop(1, SEQ, own_codes, 0)

    @pl.when(to_next)
    def _():
        def f(t, _):
            send_codes(a + 1, t, j - (SEQ - HALO), 1)
            return 0

        lax.fori_loop(0, SEQ, f, 0)

    @pl.when(to_prev)
    def _():
        def f(t, _):
            send_codes(a - 1, t, j + SEQ + HALO, 2)
            return 0

        lax.fori_loop(0, SEQ, f, 0)

    codes[j + HALO] = sendc[h]
    outside = jnp.where(lax.broadcasted_iota(I32, (HALO, 8, 128), 1) < 4, VOCAB, 0)

    @pl.when(a == 0)
    def _():
        codes[0:HALO] = outside

    @pl.when(a == CTX - 1)
    def _():
        codes[SEQ + HALO : SLOTS] = outside

    for i in range(4, 8):
        widen(i)

    def code_wait(count, sem):
        view = codes.at[pl.ds(0, count)]
        pltpu.make_async_copy(view, view, sem).wait()

    code_wait(SEQ - 1, crecv_sem.at[0])

    @pl.when(a > 0)
    def _():
        code_wait(HALO, crecv_sem.at[1])

    @pl.when(a < CTX - 1)
    def _():
        code_wait(HALO, crecv_sem.at[2])

    lanes = lax.broadcasted_iota(I32, (BLOCKS // 2, 128), 1)
    for s in range(2):
        for v in range(2):
            def bottom(beta):
                d, u = divmod(beta, 2)
                return codes[d : d + BLOCKS // 2, 2 * s + u, :]

            def upper(beta):
                d, u = divmod(beta, 2)
                x = codes[d : d + BLOCKS // 2, 4 + s, :]
                if u:
                    y = codes[d + 1 : d + 1 + BLOCKS // 2, 4 + s, :]
                    x = jnp.where(lanes < 64, x, y)
                return x, 32 * u

            lead = v + 2 * HALO
            before, after = lead - DIL_BLOCKS, lead + DIL_BLOCKS
            left = jnp.where(lanes >= 128 - DIL_REST, bottom(before - 1), bottom(before))
            right = jnp.where(lanes < DIL_REST, bottom(after + 1), bottom(after))
            up_own, own0 = upper(lead)
            up_left, left0 = upper(before - 1)
            up_right, right0 = upper(after)
            row = None
            for x, lane0, first, step in (
                (bottom(lead), OWN, 0, COLS),
                (left, LEFT, -DIL_REST, COLS),
                (right, RIGHT, DIL_REST, COLS),
                (up_own, COND + OWN, own0, 2),
                (up_left, COND + LEFT, left0 + 32 - 3, 2),
                (up_right, COND + RIGHT, right0 + 2, 2),
            ):
                amount = lax.rem(lane0 - first + 256 - step * k, 128)
                rolled = pltpu.roll(x, amount, 1)
                row = rolled if row is None else jnp.where(lanes >= lane0, rolled, row)
            gath[pl.ds(s * BLOCKS + v, BLOCKS // 2, stride=2), :] = row
    to_smem = pltpu.make_async_copy(gath, gsm, g_sem)
    to_smem.start()
    to_smem.wait()

    scale = 1.0 / math.sqrt(ATTN)
    half = CHUNK // 2
    ri = lax.broadcasted_iota(I32, (half, half), 0)
    ci = lax.broadcasted_iota(I32, (half, half), 1)
    allowed = jnp.logical_and(ri // BLOCKS == ci // BLOCKS, ci <= ri)

    def gather_rows(s):
        def gather(b, _):
            r = s * BLOCKS + b
            for t, (lane0, conds) in enumerate(TAPS):
                upper = [
                    tc[pl.ds(gsm[r, COND + lane0 + c] * 8, 8), :] for c in range(max(conds) + 1)
                ]
                for c in range(COLS):
                    x = tb[pl.ds(gsm[r, lane0 + c] * 8, 8), :] + upper[conds[c]]
                    act[t, pl.ds(c * BLOCKS + b, 8, stride=PITCH), :] = x
            return 0

        lax.fori_loop(0, BLOCKS, gather, 0, unroll=2)

    def pack_rows(s):
        def pack(i, _):
            for t in range(3):
                for g in range(GROUPS):
                    x = act[t, pl.ds(g * PITCH + i * 64, 64), :]
                    lhs[pl.ds(i * 64, 64), t * CH + g * 128 : t * CH + (g + 1) * 128] = (
                        jnp.maximum(x, 0.0).astype(BF16)
                    )
            return 0

        lax.fori_loop(0, CHUNK // 64, pack, 0)

    def ready(s, i):
        if s == 0:
            weights[i].wait()

    def convolve(s):
        ready(s, 0)
        for n in range(CH // 512):
            acc = jnp.dot(
                lhs[...], wconv[:, n * 512 : (n + 1) * 512], preferred_element_type=F32
            )
            hidden[:, n * 512 : (n + 1) * 512] = jnp.maximum(acc, 0.0).astype(BF16)

    def mix_rows(s):
        ready(s, 1)
        for n in range(CH // 512):
            acc = jnp.dot(
                hidden[...], wmix[:, n * 512 : (n + 1) * 512], preferred_element_type=F32
            )
            for g in range(4):
                stream = act[1, pl.ds((4 * n + g) * PITCH, CHUNK), :]
                resid[:, n * 512 + g * 128 : n * 512 + (g + 1) * 128] = (
                    stream + acc[:, g * 128 : (g + 1) * 128]
                ).astype(BF16)

    def project(s):
        ready(s, 2)
        for n0, n1 in ((0, 512), (512, 1024), (1024, 1536), (1536, WIDTH)):
            pj[:, n0:n1] = jnp.dot(resid[...], wproj[:, n0:n1], preferred_element_type=F32)

    def normalise(s):
        def norm(i, _):
            x = pj[pl.ds(i * 64, 64), :]
            x = x - jnp.mean(x, axis=-1, keepdims=True)
            var = jnp.mean(x * x, axis=-1, keepdims=True)
            x = x * lax.rsqrt(var + 1e-05)
            for g in range(WIDTH // 128):
                y = x[:, g * 128 : (g + 1) * 128] * gain_ref[g : g + 1, :] + bias_ref[g : g + 1, :]
                normed[pl.ds(i * 64, 64), g * 128 : (g + 1) * 128] = y.astype(BF16)
            return 0

        lax.fori_loop(0, CHUNK // 64, norm, 0)

    def make_qkv(s):
        ready(s, 3)
        for n in range(3):
            qkv[n] = lax.dot_general(
                normed[...],
                wattn[n * ATTN : (n + 1) * ATTN, :],
                (((1,), (1,)), ((), ())),
                preferred_element_type=F32,
            ).astype(BF16)

    def attend(s):
        for p in range(2):
            rows = slice(p * half, (p + 1) * half)
            query = qkv[0, rows, :]
            keys = qkv[1, rows, :]
            values = qkv[2, rows, :]
            scores = lax.dot_general(
                query, keys, (((1,), (1,)), ((), ())), preferred_element_type=F32
            ) * scale
            scores = jnp.where(allowed, scores, -jnp.inf)
            e = jnp.exp(scores - jnp.max(scores, axis=-1, keepdims=True))
            w = (e * (1.0 / jnp.sum(e, axis=-1, keepdims=True))).astype(BF16)
            mixed = jnp.dot(w, values, preferred_element_type=F32)
            for g in range(4):
                wide = min(128, ATTN - g * 128)
                for c in range(COLS // 2):
                    att[g, pl.ds((p * COLS // 2 + c) * CPITCH, BLOCKS), 0:wide] = mixed[
                        c * BLOCKS : (c + 1) * BLOCKS, g * 128 : g * 128 + wide
                    ]

    def regroup_rows(s):
        def regroup(i, _):
            for v in range(2):
                for g in range(4):
                    x = att[g, pl.ds(2 * i + v, COLS, stride=CPITCH), :]
                    wide = min(128, ATTN - g * 128)
                    sendo[s, i, v * COLS : (v + 1) * COLS, g * 128 : g * 128 + wide] = x[
                        :, :wide
                    ].astype(BF16)
            return 0

        lax.fori_loop(0, SEQ, regroup, 0, unroll=2)

    def send_rows(s):
        song = 2 * h + s

        def send_out(t, _):
            peer = lax.rem(j + t, SEQ)
            pltpu.make_async_remote_copy(
                src_ref=sendo.at[s, peer],
                dst_ref=out_ref.at[song, k],
                send_sem=osend_sem.at[s],
                recv_sem=orecv_sem.at[s],
                device_id=(a, peer),
                device_id_type=MESH,
            ).start()
            return 0

        lax.fori_loop(1, SEQ, send_out, 0)
        pltpu.make_async_copy(sendo.at[s, j], out_ref.at[song, k], local_sem.at[s]).start()

    for s in range(2):
        gather_rows(s)
        pack_rows(s)
        convolve(s)
        mix_rows(s)
        project(s)
        normalise(s)
        make_qkv(s)
        attend(s)
        regroup_rows(s)
        send_rows(s)

    for s in range(2):
        view = sendo.at[s, pl.ds(0, SEQ - 1)]
        pltpu.make_async_copy(view, view, osend_sem.at[s]).wait()
        pltpu.make_async_copy(view, view, orecv_sem.at[s]).wait()
        pltpu.make_async_copy(sendo.at[s, j], out_ref.at[2 * h + s, k], local_sem.at[s]).wait()
    code_wait(SEQ - 1, csend_sem)

    @pl.when(jnp.logical_or(to_next, to_prev))
    def _():
        code_wait(SEQ, csend_sem)


def body(
    bottom_codes, cond_codes, bottom_table, cond_table, conv_dilated, conv_mix,
    projection, norm_gain, norm_bias, attn_weight,
):
    vmem = pl.BlockSpec(memory_space=pltpu.VMEM)
    hbm = pl.BlockSpec(memory_space=pl.ANY)
    dma = pltpu.SemaphoreType.DMA
    out = pl.pallas_call(
        kernel,
        out_shape=jax.ShapeDtypeStruct((4, SEQ // 2, 16, ATTN), BF16),
        in_specs=[vmem] * 4 + [hbm] * 6,
        out_specs=hbm,
        scratch_shapes=[
            pltpu.VMEM((VOCAB * 8 + 8, 128), F32),
            pltpu.VMEM((VOCAB * 8, 128), F32),
            pltpu.VMEM((4, STAGE, CH), BF16),
            pltpu.VMEM((3 * CH, CH), BF16),
            pltpu.VMEM((CH, CH), BF16),
            pltpu.VMEM((CH, WIDTH), BF16),
            pltpu.VMEM((3 * ATTN, WIDTH), BF16),
            pltpu.VMEM((2, 8, 128), I32),
            pltpu.VMEM((SLOTS, 8, 128), I32),
            pltpu.VMEM((2 * BLOCKS, 128), I32),
            pltpu.SMEM((2 * BLOCKS, 128), I32),
            pltpu.VMEM((3, GROUPS * PITCH, 128), F32),
            pltpu.VMEM((CHUNK, 3 * CH), BF16),
            pltpu.VMEM((CHUNK, CH), BF16),
            pltpu.VMEM((CHUNK, CH), BF16),
            pltpu.VMEM((CHUNK, WIDTH), F32),
            pltpu.VMEM((CHUNK, WIDTH), BF16),
            pltpu.VMEM((3, CHUNK, ATTN), BF16),
            pltpu.VMEM((4, COLS * CPITCH, 128), F32),
            pltpu.VMEM((2, SEQ, 16, ATTN), BF16),
            dma((4,)),
            dma((4,)),
            dma,
            dma((3,)),
            dma,
            dma((2,)),
            dma((2,)),
            dma((2,)),
        ],
        compiler_params=pltpu.CompilerParams(
            collective_id=0, has_side_effects=True, vmem_limit_bytes=63 * 1024 * 1024
        ),
        cost_estimate=pl.CostEstimate(
            flops=18_300_000_000, bytes_accessed=28_000_000, transcendentals=300_000
        ),
        name="upsampler",
    )(
        bottom_codes, cond_codes, norm_gain.reshape(WIDTH // 128, 128),
        norm_bias.reshape(WIDTH // 128, 128),
        bottom_table, cond_table, conv_dilated.reshape(3 * CH, CH), conv_mix, projection,
        attn_weight.T,
    )
    songs = bottom_codes.shape[0]
    out = out.reshape(songs, SEQ // 2, 2, COLS, ATTN).transpose(0, 2, 1, 3, 4)
    return out.reshape(songs, ROWS, ATTN)


def solution(mesh):
    split = P(None, ("ctx", "seq"))
    return jax.shard_map(
        body,
        mesh=mesh,
        in_specs=(split, split) + (P(),) * 8,
        out_specs=P(None, ("ctx", "seq"), None),
        check_vma=False,
    )
```

```python
import functools
import math

import jax
import jax.numpy as jnp
from jax import lax
from jax.experimental import pallas as pl
from jax.experimental.pallas import tpu as pltpu
from jax.sharding import PartitionSpec as P

F32, BF16, I32 = jnp.float32, jnp.bfloat16, jnp.int32
MESH = pl.DeviceIdType.MESH

BLOCK = 128
DIL_BLOCKS, DIL_REST = divmod(2187, BLOCK)
CTX, SEQ = 4, 32
ROWS = 256
HALO = 9
SLOTS = SEQ + 2 * HALO
BLOCKS = 64
COLS = 4
CHUNK = BLOCKS * COLS
HALF = CHUNK // 2
CHUNKS = 4
VOCAB, CH, WIDTH, ATTN = 2048, 1024, 1920, 480
GROUPS = CH // 128
PITCH = CHUNK + 8
CPITCH = SEQ + 8
NOWHERE = VOCAB * 8
STAGE = 512
OWN, LEFT, RIGHT = 0, 8, 16
COND = 32
TAPS = ((LEFT, (0, 0, 0, 1)), (OWN, (0, 0, 0, 0)), (RIGHT, (0, 1, 1, 1)))


def kernel(
    bottom_ref, cond_ref, gain_ref, bias_ref, btab, ctab, conv, mix, proj, attn,
    out_ref,
    tb, tc, stage, wconv, wmix, wproj, wattn,
    sendc, codes, gath, gsm,
    stream, act, lhs, hidden, resid, pj, normed, qkv, att, sendo, got, turned,
    stage_sem, w_sem, csend_sem, crecv_sem, g_sem, osend_sem, orecv_sem, local_sem, out_sem,
):
    a = lax.axis_index("ctx")
    j = lax.axis_index("seq")
    k = j // 2
    h = j % 2

    to_next = jnp.logical_and(a < CTX - 1, j >= SEQ - HALO)
    to_prev = jnp.logical_and(a > 0, j < HALO)

    barrier = pltpu.get_barrier_semaphore()

    def greet(t, _):
        pl.semaphore_signal(
            barrier, inc=1, device_id=(a, lax.rem(j + t, SEQ)), device_id_type=MESH
        )
        return 0

    lax.fori_loop(1, SEQ, greet, 0)

    @pl.when(a > 0)
    def _():
        def f(t, _):
            pl.semaphore_signal(barrier, inc=1, device_id=(a - 1, t), device_id_type=MESH)
            return 0

        lax.fori_loop(SEQ - HALO, SEQ, f, 0)

    @pl.when(a < CTX - 1)
    def _():
        def f(t, _):
            pl.semaphore_signal(barrier, inc=1, device_id=(a + 1, t), device_id_type=MESH)
            return 0

        lax.fori_loop(0, HALO, f, 0)

    def stage_copy(i):
        table = (btab, ctab)[i // 4]
        return pltpu.make_async_copy(
            table.at[pl.ds((i % 4) * STAGE, STAGE)], stage.at[i % 4], stage_sem.at[i % 4]
        )

    weights = [
        pltpu.make_async_copy(src, dst, w_sem.at[i])
        for i, (src, dst) in enumerate(
            ((conv, wconv), (mix, wmix), (proj, wproj), (attn, wattn))
        )
    ]
    for i in range(4):
        stage_copy(i).start()

    sendc[...] = jnp.zeros_like(sendc)
    for song in range(4):
        p, s = divmod(song, 2)
        for u in range(2):
            sendc[p, 2 * s + u : 2 * s + u + 1, :] = bottom_ref[
                song : song + 1, u * 128 : (u + 1) * 128
            ]
            sendc[p, 4 + s : 5 + s, u * 64 : (u + 1) * 64] = cond_ref[song : song + 1, :]

    def widen(i):
        table = (tb, tc)[i // 4]
        stage_copy(i).wait()

        def f(r, _):
            x = stage[i % 4, pl.ds(r * 16, 16), :].astype(F32)
            base = ((i % 4) * STAGE + r * 16) * 8
            for q in range(2):
                for g in range(GROUPS):
                    table[pl.ds(base + q * 64 + g, 8, stride=8), :] = x[
                        8 * q : 8 * q + 8, 128 * g : 128 * g + 128
                    ]
            return 0

        lax.fori_loop(0, STAGE // 16, f, 0, unroll=2)
        if i + 4 < 8:
            stage_copy(i + 4).start()

    for i in range(2):
        widen(i)

    pl.semaphore_wait(barrier, SEQ - 1 + jnp.where(jnp.logical_or(to_next, to_prev), SEQ, 0))

    def send_codes(ctx, peer, slot, sem):
        pltpu.make_async_remote_copy(
            src_ref=sendc.at[peer % 2],
            dst_ref=codes.at[slot],
            send_sem=csend_sem,
            recv_sem=crecv_sem.at[sem],
            device_id=(ctx, peer),
            device_id_type=MESH,
        ).start()

    def own_codes(t, _):
        send_codes(a, lax.rem(j + t, SEQ), j + HALO, 0)
        return 0

    lax.fori_loop(1, SEQ, own_codes, 0)

    @pl.when(to_next)
    def _():
        def f(t, _):
            send_codes(a + 1, t, j - (SEQ - HALO), 1)
            return 0

        lax.fori_loop(0, SEQ, f, 0)

    @pl.when(to_prev)
    def _():
        def f(t, _):
            send_codes(a - 1, t, j + SEQ + HALO, 2)
            return 0

        lax.fori_loop(0, SEQ, f, 0)

    codes[j + HALO] = sendc[h]
    outside = jnp.where(lax.broadcasted_iota(I32, (HALO, 8, 128), 1) < 4, VOCAB, 0)

    @pl.when(a == 0)
    def _():
        codes[0:HALO] = outside

    @pl.when(a == CTX - 1)
    def _():
        codes[SEQ + HALO : SLOTS] = outside

    for i in range(2, 4):
        widen(i)
    for w in weights:
        w.start()
    tb[pl.ds(NOWHERE, 8), :] = jnp.full((8, 128), -1e9, F32)

    for i in range(4, 8):
        widen(i)

    def code_wait(count, sem):
        view = codes.at[pl.ds(0, count)]
        pltpu.make_async_copy(view, view, sem).wait()

    code_wait(SEQ - 1, crecv_sem.at[0])

    @pl.when(a > 0)
    def _():
        code_wait(HALO, crecv_sem.at[1])

    @pl.when(a < CTX - 1)
    def _():
        code_wait(HALO, crecv_sem.at[2])

    lanes = lax.broadcasted_iota(I32, (BLOCKS // 2, 128), 1)

    def to_smem(s):
        rows = pl.ds(s * SEQ, SEQ)
        return pltpu.make_async_copy(gath.at[rows], gsm.at[rows], g_sem.at[s])

    for s in range(2):
        pair = None
        for v in range(2):
            def bottom(beta):
                d, u = divmod(beta, 2)
                return codes[d : d + BLOCKS // 2, 2 * s + u, :]

            def upper(beta):
                d, u = divmod(beta, 2)
                x = codes[d : d + BLOCKS // 2, 4 + s, :]
                if u:
                    y = codes[d + 1 : d + 1 + BLOCKS // 2, 4 + s, :]
                    x = jnp.where(lanes < 64, x, y)
                return x, 32 * u

            lead = v + 2 * HALO
            before, after = lead - DIL_BLOCKS, lead + DIL_BLOCKS
            left = jnp.where(lanes >= 128 - DIL_REST, bottom(before - 1), bottom(before))
            right = jnp.where(lanes < DIL_REST, bottom(after + 1), bottom(after))
            up_own, own0 = upper(lead)
            up_left, left0 = upper(before - 1)
            up_right, right0 = upper(after)
            row = None
            for x, lane0, first, step in (
                (bottom(lead), OWN, 0, 8),
                (left, LEFT, -DIL_REST, 8),
                (right, RIGHT, DIL_REST, 8),
                (up_own, COND + OWN, own0, 2),
                (up_left, COND + LEFT, left0 + 32 - 3, 2),
                (up_right, COND + RIGHT, right0 + 2, 2),
            ):
                lane0 += 64 * v
                amount = lax.rem(lane0 - first + 256 - step * k, 128)
                rolled = pltpu.roll(x, amount, 1)
                row = rolled if row is None else jnp.where(lanes >= lane0, rolled, row)
            pair = row if pair is None else jnp.where(lanes < 64, pair, row)
        gath[s * SEQ : (s + 1) * SEQ, :] = pair * 8
        to_smem(s).start()
    to_smem(0).wait()

    scale = 1.0 / math.sqrt(ATTN)
    ri = lax.broadcasted_iota(I32, (CHUNK, CHUNK), 0)
    ci = lax.broadcasted_iota(I32, (CHUNK, CHUNK), 1)
    allowed = jnp.logical_and(
        (ri // SEQ) % COLS == (ci // SEQ) % COLS,
        2 * (ci % SEQ) + ci // HALF <= 2 * (ri % SEQ) + ri // HALF,
    )

    def gather_rows(i, first, count):
        s, p = divmod(i, 2)
        for q in range(count):
            b = first + q
            r, at = s * SEQ + b // 2, (q % 2) * 64
            row = b // 2 + (q % 2) * HALF
            for t, (lane0, conds) in enumerate(TAPS):
                upper = [
                    tc[pl.ds(gsm[r, at + COND + lane0 + p + c], 8), :]
                    for c in range(max(conds) + 1)
                ]
                for c in range(COLS):
                    x = tb[pl.ds(gsm[r, at + lane0 + COLS * p + c], 8), :] + upper[conds[c]]
                    if t == 1:
                        stream[i % 2, pl.ds(row + c * SEQ, 8, stride=PITCH), :] = x
                    else:
                        act[t // 2, pl.ds(row + c * SEQ, 8, stride=PITCH), :] = x

    def pack_rows(i, first, count):
        for t in range(3):
            for g in range(GROUPS):
                rows = pl.ds(g * PITCH + first, count)
                x = stream[i % 2, rows, :] if t == 1 else act[t // 2, rows, :]
                lhs[first : first + count, t * CH + g * 128 : t * CH + (g + 1) * 128] = (
                    jnp.maximum(x, 0.0).astype(BF16)
                )

    def convolve(i, n):
        cols = slice(n * 256, (n + 1) * 256)
        acc = jnp.dot(lhs[...], wconv[:, cols], preferred_element_type=F32)
        hidden[:, cols] = jnp.maximum(acc, 0.0).astype(BF16)

    def mix_rows(i):
        for n in range(CH // 256):
            acc = jnp.dot(
                hidden[...], wmix[:, n * 256 : (n + 1) * 256], preferred_element_type=F32
            )
            for g in range(2):
                own = stream[i % 2, pl.ds((2 * n + g) * PITCH, CHUNK), :]
                resid[:, n * 256 + g * 128 : n * 256 + (g + 1) * 128] = (
                    own + acc[:, g * 128 : (g + 1) * 128]
                ).astype(BF16)

    def project(n0, n1):
        pj[:, n0:n1] = jnp.dot(resid[...], wproj[:, n0:n1], preferred_element_type=F32)

    def normalise(first, count):
        rows = slice(first, first + count)
        x = pj[rows, :]
        x = x - jnp.mean(x, axis=-1, keepdims=True)
        var = jnp.mean(x * x, axis=-1, keepdims=True)
        x = x * lax.rsqrt(var + 1e-05)
        for g in range(WIDTH // 128):
            y = x[:, g * 128 : (g + 1) * 128] * gain_ref[g : g + 1, :] + bias_ref[g : g + 1, :]
            normed[rows, g * 128 : (g + 1) * 128] = y.astype(BF16)

    def make_qkv(n):
        qkv[n] = lax.dot_general(
            normed[...],
            wattn[n * ATTN : (n + 1) * ATTN, :],
            (((1,), (1,)), ((), ())),
            preferred_element_type=F32,
        ).astype(BF16)

    def attend():
        scores = lax.dot_general(
            qkv[0], qkv[1], (((1,), (1,)), ((), ())), preferred_element_type=F32
        ) * scale
        scores = jnp.where(allowed, scores, -jnp.inf)
        e = jnp.exp(scores - jnp.max(scores, axis=-1, keepdims=True))
        w = (e * (1.0 / jnp.sum(e, axis=-1, keepdims=True))).astype(BF16)
        mixed = jnp.dot(w, qkv[2], preferred_element_type=F32)
        for g in range(4):
            wide = min(128, ATTN - g * 128)
            for c in range(8):
                att[g, c * CPITCH : c * CPITCH + SEQ, 0:wide] = mixed[
                    c * SEQ : (c + 1) * SEQ, g * 128 : g * 128 + wide
                ]

    def regroup_rows(i):
        def regroup(d, _):
            for g in range(4):
                x = att[g, pl.ds(d, 8, stride=CPITCH), :]
                wide = min(128, ATTN - g * 128)
                sendo[i, d, :, g * 128 : g * 128 + wide] = x[:, :wide].astype(BF16)
            return 0

        lax.fori_loop(0, SEQ, regroup, 0, unroll=8)

    def send_rows(i):
        s, p = divmod(i, 2)
        song = 2 * h + s

        def send_out(t, _):
            peer = lax.rem(j + t, SEQ)
            pltpu.make_async_remote_copy(
                src_ref=sendo.at[i, peer],
                dst_ref=got.at[song, k, p],
                send_sem=osend_sem.at[i],
                recv_sem=orecv_sem.at[i],
                device_id=(a, peer),
                device_id_type=MESH,
            ).start()
            return 0

        lax.fori_loop(1, SEQ, send_out, 0)
        pltpu.make_async_copy(sendo.at[i, j], got.at[song, k, p], local_sem.at[i]).start()

    def first_rows(e, _):
        gather_rows(0, e * 4, 4)
        return 0

    lax.fori_loop(0, BLOCKS // 4, first_rows, 0)
    for q in range(4):
        pack_rows(0, q * 64, 64)

    for i in range(CHUNKS):
        if i == 0:
            weights[0].wait()

        for n in range(CH // 256):
            convolve(i, n)
            if i + 1 < CHUNKS:
                gather_rows(i + 1, n * 16, 16)
        if i == 0:
            weights[1].wait()
        mix_rows(i)
        if i == 0:
            weights[2].wait()
        for q, (n0, n1) in enumerate(((0, 512), (512, 1024), (1024, 1536), (1536, WIDTH))):
            project(n0, n1)
            if i + 1 < CHUNKS:
                pack_rows(i + 1, q * 64, 64)
        normalise(0, CHUNK)
        if i == 0:
            weights[3].wait()
            to_smem(1).wait()
        for n in range(3):
            make_qkv(n)
        attend()
        regroup_rows(i)
        send_rows(i)

    ri = lax.broadcasted_iota(I32, (ROWS, ROWS), 0)
    ci = lax.broadcasted_iota(I32, (ROWS, ROWS), 1)
    place = (ri // 8) * COLS + ri % COLS + ((ri // COLS) % 2) * BLOCK
    order = jnp.where(place == ci, 1.0, 0.0).astype(BF16)
    out_copies = []
    for s in range(2):
        for i in (2 * s, 2 * s + 1):
            view = sendo.at[i, pl.ds(0, SEQ - 1)]
            pltpu.make_async_copy(view, view, osend_sem.at[i]).wait()
            pltpu.make_async_copy(view, view, orecv_sem.at[i]).wait()
            pltpu.make_async_copy(
                sendo.at[i, j], got.at[2 * h + s, k, i % 2], local_sem.at[i]
            ).wait()
        for song in (s, s + 2):
            x = got[song].astype(F32).reshape(ROWS, ATTN).astype(BF16)
            turned[song] = lax.dot_general(
                x, order, (((0,), (0,)), ((), ())), preferred_element_type=F32
            ).astype(BF16)
            copy = pltpu.make_async_copy(turned.at[song], out_ref.at[song], out_sem.at[song])
            copy.start()
            out_copies.append(copy)
    for copy in out_copies:
        copy.wait()
    code_wait(SEQ - 1, csend_sem)

    @pl.when(jnp.logical_or(to_next, to_prev))
    def _():
        code_wait(SEQ, csend_sem)


def body(
    bottom_codes, cond_codes, bottom_table, cond_table, conv_dilated, conv_mix,
    projection, norm_gain, norm_bias, attn_weight,
):
    vmem = pl.BlockSpec(memory_space=pltpu.VMEM)
    hbm = pl.BlockSpec(memory_space=pl.ANY)
    dma = pltpu.SemaphoreType.DMA
    out = pl.pallas_call(
        kernel,
        out_shape=jax.ShapeDtypeStruct((4, ATTN, ROWS), BF16),
        in_specs=[vmem] * 4 + [hbm] * 6,
        out_specs=hbm,
        scratch_shapes=[
            pltpu.VMEM((VOCAB * 8 + 8, 128), F32),
            pltpu.VMEM((VOCAB * 8, 128), F32),
            pltpu.VMEM((4, STAGE, CH), BF16),
            pltpu.VMEM((3 * CH, CH), BF16),
            pltpu.VMEM((CH, CH), BF16),
            pltpu.VMEM((CH, WIDTH), BF16),
            pltpu.VMEM((3 * ATTN, WIDTH), BF16),
            pltpu.VMEM((2, 8, 128), I32),
            pltpu.VMEM((SLOTS, 8, 128), I32),
            pltpu.VMEM((BLOCKS, 128), I32),
            pltpu.SMEM((BLOCKS, 128), I32),
            pltpu.VMEM((2, GROUPS * PITCH, 128), F32),
            pltpu.VMEM((2, GROUPS * PITCH, 128), F32),
            pltpu.VMEM((CHUNK, 3 * CH), BF16),
            pltpu.VMEM((CHUNK, CH), BF16),
            pltpu.VMEM((CHUNK, CH), BF16),
            pltpu.VMEM((CHUNK, WIDTH), F32),
            pltpu.VMEM((CHUNK, WIDTH), BF16),
            pltpu.VMEM((3, CHUNK, ATTN), BF16),
            pltpu.VMEM((4, 8 * CPITCH, 128), F32),
            pltpu.VMEM((CHUNKS, SEQ, 8, ATTN), BF16),
            pltpu.VMEM((4, SEQ // 2, 2, 8, ATTN), BF16),
            pltpu.VMEM((4, ATTN, ROWS), BF16),
            dma((4,)),
            dma((4,)),
            dma,
            dma((3,)),
            dma((2,)),
            dma((CHUNKS,)),
            dma((CHUNKS,)),
            dma((CHUNKS,)),
            dma((4,)),
        ],
        compiler_params=pltpu.CompilerParams(
            collective_id=0, has_side_effects=True, vmem_limit_bytes=63 * 1024 * 1024
        ),
        cost_estimate=pl.CostEstimate(
            flops=18_300_000_000, bytes_accessed=28_000_000, transcendentals=300_000
        ),
        name="upsampler",
    )(
        bottom_codes, cond_codes, norm_gain.reshape(WIDTH // 128, 128),
        norm_bias.reshape(WIDTH // 128, 128),
        bottom_table, cond_table, conv_dilated.reshape(3 * CH, CH), conv_mix, projection,
        attn_weight.T,
    )
    return out.transpose(0, 2, 1)


def solution(mesh):
    split = P(None, ("ctx", "seq"))
    return jax.shard_map(
        body,
        mesh=mesh,
        in_specs=(split, split) + (P(),) * 8,
        out_specs=P(None, ("ctx", "seq"), None),
        check_vma=False,
    )
```

```python
import functools
import math

import jax
import jax.numpy as jnp
from jax import lax
from jax.experimental import pallas as pl
from jax.experimental.pallas import tpu as pltpu
from jax.sharding import PartitionSpec as P

F32, BF16, I32 = jnp.float32, jnp.bfloat16, jnp.int32
MESH = pl.DeviceIdType.MESH

BLOCK = 128
DIL_BLOCKS, DIL_REST = divmod(2187, BLOCK)
CTX, SEQ = 4, 32
ROWS = 256
HALO = 9
SLOTS = SEQ + 2 * HALO
BLOCKS = 64
COLS = 4
CHUNK = BLOCKS * COLS
HALF = CHUNK // 2
CHUNKS = 4
VOCAB, CH, WIDTH, ATTN = 2048, 1024, 1920, 480
GROUPS = CH // 128
PITCH = CHUNK + 8
CPITCH = SEQ + 8
NOWHERE = VOCAB * 8
STAGE = 512
OWN, LEFT, RIGHT = 0, 8, 16
COND = 32
TAPS = ((LEFT, (0, 0, 0, 1)), (OWN, (0, 0, 0, 0)), (RIGHT, (0, 1, 1, 1)))


def kernel(
    bottom_ref, cond_ref, gain_ref, bias_ref, btab, ctab, conv, mix, proj, attn,
    out_ref,
    tb, tc, stage, wconv, wmix, wproj, wattn,
    sendc, codes, gath, gsm,
    stream, act, lhs, hidden, resid, pj, normed, qkv, att, sendo, got,
    stage_sem, w_sem, csend_sem, crecv_sem, g_sem, osend_sem, orecv_sem, local_sem,
):
    a = lax.axis_index("ctx")
    j = lax.axis_index("seq")
    k = j // 2
    h = j % 2

    to_next = jnp.logical_and(a < CTX - 1, j >= SEQ - HALO)
    to_prev = jnp.logical_and(a > 0, j < HALO)

    barrier = pltpu.get_barrier_semaphore()

    def greet(t, _):
        pl.semaphore_signal(
            barrier, inc=1, device_id=(a, lax.rem(j + t, SEQ)), device_id_type=MESH
        )
        return 0

    lax.fori_loop(1, SEQ, greet, 0)

    @pl.when(a > 0)
    def _():
        def f(t, _):
            pl.semaphore_signal(barrier, inc=1, device_id=(a - 1, t), device_id_type=MESH)
            return 0

        lax.fori_loop(SEQ - HALO, SEQ, f, 0)

    @pl.when(a < CTX - 1)
    def _():
        def f(t, _):
            pl.semaphore_signal(barrier, inc=1, device_id=(a + 1, t), device_id_type=MESH)
            return 0

        lax.fori_loop(0, HALO, f, 0)

    def stage_copy(i):
        table = (btab, ctab)[i // 4]
        return pltpu.make_async_copy(
            table.at[pl.ds((i % 4) * STAGE, STAGE)], stage.at[i % 4], stage_sem.at[i % 4]
        )

    weights = [
        pltpu.make_async_copy(src, dst, w_sem.at[i])
        for i, (src, dst) in enumerate(
            ((conv, wconv), (mix, wmix), (proj, wproj), (attn, wattn))
        )
    ]
    for i in range(4):
        stage_copy(i).start()

    sendc[...] = jnp.zeros_like(sendc)
    for song in range(4):
        p, s = divmod(song, 2)
        for u in range(2):
            sendc[p, 2 * s + u : 2 * s + u + 1, :] = bottom_ref[
                song : song + 1, u * 128 : (u + 1) * 128
            ]
            sendc[p, 4 + s : 5 + s, u * 64 : (u + 1) * 64] = cond_ref[song : song + 1, :]

    def widen(i):
        table = (tb, tc)[i // 4]
        stage_copy(i).wait()

        def f(r, _):
            x = stage[i % 4, pl.ds(r * 16, 16), :].astype(F32)
            base = ((i % 4) * STAGE + r * 16) * 8
            for q in range(2):
                for g in range(GROUPS):
                    table[pl.ds(base + q * 64 + g, 8, stride=8), :] = x[
                        8 * q : 8 * q + 8, 128 * g : 128 * g + 128
                    ]
            return 0

        lax.fori_loop(0, STAGE // 16, f, 0, unroll=2)
        if i + 4 < 8:
            stage_copy(i + 4).start()

    for i in range(2):
        widen(i)

    pl.semaphore_wait(barrier, SEQ - 1 + jnp.where(jnp.logical_or(to_next, to_prev), SEQ, 0))

    def send_codes(ctx, peer, slot, sem):
        pltpu.make_async_remote_copy(
            src_ref=sendc.at[peer % 2],
            dst_ref=codes.at[slot],
            send_sem=csend_sem,
            recv_sem=crecv_sem.at[sem],
            device_id=(ctx, peer),
            device_id_type=MESH,
        ).start()

    def own_codes(t, _):
        send_codes(a, lax.rem(j + t, SEQ), j + HALO, 0)
        return 0

    lax.fori_loop(1, SEQ, own_codes, 0)

    @pl.when(to_next)
    def _():
        def f(t, _):
            send_codes(a + 1, t, j - (SEQ - HALO), 1)
            return 0

        lax.fori_loop(0, SEQ, f, 0)

    @pl.when(to_prev)
    def _():
        def f(t, _):
            send_codes(a - 1, t, j + SEQ + HALO, 2)
            return 0

        lax.fori_loop(0, SEQ, f, 0)

    codes[j + HALO] = sendc[h]
    outside = jnp.where(lax.broadcasted_iota(I32, (HALO, 8, 128), 1) < 4, VOCAB, 0)

    @pl.when(a == 0)
    def _():
        codes[0:HALO] = outside

    @pl.when(a == CTX - 1)
    def _():
        codes[SEQ + HALO : SLOTS] = outside

    for i in range(2, 4):
        widen(i)
    for w in weights:
        w.start()
    tb[pl.ds(NOWHERE, 8), :] = jnp.full((8, 128), -1e9, F32)

    for i in range(4, 8):
        widen(i)

    def code_wait(count, sem):
        view = codes.at[pl.ds(0, count)]
        pltpu.make_async_copy(view, view, sem).wait()

    code_wait(SEQ - 1, crecv_sem.at[0])

    @pl.when(a > 0)
    def _():
        code_wait(HALO, crecv_sem.at[1])

    @pl.when(a < CTX - 1)
    def _():
        code_wait(HALO, crecv_sem.at[2])

    lanes = lax.broadcasted_iota(I32, (BLOCKS // 2, 128), 1)

    def to_smem(s):
        rows = pl.ds(s * SEQ, SEQ)
        return pltpu.make_async_copy(gath.at[rows], gsm.at[rows], g_sem.at[s])

    for s in range(2):
        pair = None
        for v in range(2):
            def bottom(beta):
                d, u = divmod(beta, 2)
                return codes[d : d + BLOCKS // 2, 2 * s + u, :]

            def upper(beta):
                d, u = divmod(beta, 2)
                x = codes[d : d + BLOCKS // 2, 4 + s, :]
                if u:
                    y = codes[d + 1 : d + 1 + BLOCKS // 2, 4 + s, :]
                    x = jnp.where(lanes < 64, x, y)
                return x, 32 * u

            lead = v + 2 * HALO
            before, after = lead - DIL_BLOCKS, lead + DIL_BLOCKS
            left = jnp.where(lanes >= 128 - DIL_REST, bottom(before - 1), bottom(before))
            right = jnp.where(lanes < DIL_REST, bottom(after + 1), bottom(after))
            up_own, own0 = upper(lead)
            up_left, left0 = upper(before - 1)
            up_right, right0 = upper(after)
            row = None
            for x, lane0, first, step in (
                (bottom(lead), OWN, 0, 8),
                (left, LEFT, -DIL_REST, 8),
                (right, RIGHT, DIL_REST, 8),
                (up_own, COND + OWN, own0, 2),
                (up_left, COND + LEFT, left0 + 32 - 3, 2),
                (up_right, COND + RIGHT, right0 + 2, 2),
            ):
                lane0 += 64 * v
                amount = lax.rem(lane0 - first + 256 - step * k, 128)
                rolled = pltpu.roll(x, amount, 1)
                row = rolled if row is None else jnp.where(lanes >= lane0, rolled, row)
            pair = row if pair is None else jnp.where(lanes < 64, pair, row)
        gath[s * SEQ : (s + 1) * SEQ, :] = pair * 8
        to_smem(s).start()
    to_smem(0).wait()

    scale = 1.0 / math.sqrt(ATTN)
    ri = lax.broadcasted_iota(I32, (CHUNK, CHUNK), 0)
    ci = lax.broadcasted_iota(I32, (CHUNK, CHUNK), 1)
    allowed = jnp.logical_and(
        (ri // SEQ) % COLS == (ci // SEQ) % COLS,
        2 * (ci % SEQ) + ci // HALF <= 2 * (ri % SEQ) + ri // HALF,
    )

    def gather_rows(i, first, count):
        s, p = divmod(i, 2)
        for q in range(count):
            b = first + q
            r, at = s * SEQ + b // 2, (q % 2) * 64
            row = b // 2 + (q % 2) * HALF
            for t, (lane0, conds) in enumerate(TAPS):
                upper = [
                    tc[pl.ds(gsm[r, at + COND + lane0 + p + c], 8), :]
                    for c in range(max(conds) + 1)
                ]
                for c in range(COLS):
                    x = tb[pl.ds(gsm[r, at + lane0 + COLS * p + c], 8), :] + upper[conds[c]]
                    if t == 1:
                        stream[i % 2, pl.ds(row + c * SEQ, 8, stride=PITCH), :] = x
                    else:
                        act[t // 2, pl.ds(row + c * SEQ, 8, stride=PITCH), :] = x

    def pack_rows(i, first, count):
        for t in range(3):
            for g in range(GROUPS):
                rows = pl.ds(g * PITCH + first, count)
                x = stream[i % 2, rows, :] if t == 1 else act[t // 2, rows, :]
                lhs[first : first + count, t * CH + g * 128 : t * CH + (g + 1) * 128] = (
                    jnp.maximum(x, 0.0).astype(BF16)
                )

    def convolve(i, n):
        cols = slice(n * 256, (n + 1) * 256)
        acc = jnp.dot(lhs[...], wconv[:, cols], preferred_element_type=F32)
        hidden[:, cols] = jnp.maximum(acc, 0.0).astype(BF16)

    def mix_rows(i):
        for n in range(CH // 256):
            acc = jnp.dot(
                hidden[...], wmix[:, n * 256 : (n + 1) * 256], preferred_element_type=F32
            )
            for g in range(2):
                own = stream[i % 2, pl.ds((2 * n + g) * PITCH, CHUNK), :]
                resid[:, n * 256 + g * 128 : n * 256 + (g + 1) * 128] = (
                    own + acc[:, g * 128 : (g + 1) * 128]
                ).astype(BF16)

    def project(n0, n1):
        pj[:, n0:n1] = jnp.dot(resid[...], wproj[:, n0:n1], preferred_element_type=F32)

    def normalise(first, count):
        rows = slice(first, first + count)
        x = pj[rows, :]
        x = x - jnp.mean(x, axis=-1, keepdims=True)
        var = jnp.mean(x * x, axis=-1, keepdims=True)
        x = x * lax.rsqrt(var + 1e-05)
        for g in range(WIDTH // 128):
            y = x[:, g * 128 : (g + 1) * 128] * gain_ref[g : g + 1, :] + bias_ref[g : g + 1, :]
            normed[rows, g * 128 : (g + 1) * 128] = y.astype(BF16)

    def make_qkv(n):
        qkv[n] = lax.dot_general(
            normed[...],
            wattn[n * ATTN : (n + 1) * ATTN, :],
            (((1,), (1,)), ((), ())),
            preferred_element_type=F32,
        ).astype(BF16)

    def attend():
        scores = lax.dot_general(
            qkv[0], qkv[1], (((1,), (1,)), ((), ())), preferred_element_type=F32
        ) * scale
        scores = jnp.where(allowed, scores, -jnp.inf)
        e = jnp.exp(scores - jnp.max(scores, axis=-1, keepdims=True))
        w = (e * (1.0 / jnp.sum(e, axis=-1, keepdims=True))).astype(BF16)
        mixed = jnp.dot(w, qkv[2], preferred_element_type=F32)
        for g in range(4):
            wide = min(128, ATTN - g * 128)
            for c in range(8):
                att[g, c * CPITCH : c * CPITCH + SEQ, 0:wide] = mixed[
                    c * SEQ : (c + 1) * SEQ, g * 128 : g * 128 + wide
                ]

    def regroup_rows(i):
        def regroup(d, _):
            for g in range(4):
                x = att[g, pl.ds(d, 8, stride=CPITCH), :]
                wide = min(128, ATTN - g * 128)
                sendo[i, d, :, g * 128 : g * 128 + wide] = x[:, :wide].astype(BF16)
            return 0

        lax.fori_loop(0, SEQ, regroup, 0, unroll=True)

    def send_rows(i):
        s, p = divmod(i, 2)
        song = 2 * h + s

        def send_out(t, _):
            peer = lax.rem(j + t, SEQ)
            pltpu.make_async_remote_copy(
                src_ref=sendo.at[i, peer],
                dst_ref=got.at[song, k, p],
                send_sem=osend_sem.at[i],
                recv_sem=orecv_sem.at[i],
                device_id=(a, peer),
                device_id_type=MESH,
            ).start()
            return 0

        lax.fori_loop(1, SEQ, send_out, 0)
        pltpu.make_async_copy(sendo.at[i, j], got.at[song, k, p], local_sem.at[i]).start()

    def first_rows(e, _):
        gather_rows(0, e * 4, 4)
        return 0

    lax.fori_loop(0, BLOCKS // 4, first_rows, 0)
    for q in range(4):
        pack_rows(0, q * 64, 64)

    for i in range(CHUNKS):
        if i == 0:
            weights[0].wait()

        for n in range(CH // 256):
            convolve(i, n)
            if i + 1 < CHUNKS:
                gather_rows(i + 1, n * 16, 16)
        if i == 0:
            weights[1].wait()
        mix_rows(i)
        if i == 0:
            weights[2].wait()
        for q, (n0, n1) in enumerate(((0, 512), (512, 1024), (1024, 1536), (1536, WIDTH))):
            project(n0, n1)
            if i + 1 < CHUNKS:
                pack_rows(i + 1, q * 64, 64)
        normalise(0, CHUNK)
        if i == 0:
            weights[3].wait()
            to_smem(1).wait()
        for n in range(3):
            make_qkv(n)
        attend()
        regroup_rows(i)
        send_rows(i)

    ri = lax.broadcasted_iota(I32, (ROWS, ROWS), 0)
    ci = lax.broadcasted_iota(I32, (ROWS, ROWS), 1)
    place = (ri // 8) * COLS + ri % COLS + ((ri // COLS) % 2) * BLOCK
    order = jnp.where(place == ci, 1.0, 0.0).astype(BF16)
    for s in range(2):
        for i in (2 * s, 2 * s + 1):
            view = sendo.at[i, pl.ds(0, SEQ - 1)]
            pltpu.make_async_copy(view, view, osend_sem.at[i]).wait()
            pltpu.make_async_copy(view, view, orecv_sem.at[i]).wait()
            pltpu.make_async_copy(
                sendo.at[i, j], got.at[2 * h + s, k, i % 2], local_sem.at[i]
            ).wait()
        for song in (s, s + 2):
            x = got[song].astype(F32).reshape(ROWS, ATTN).astype(BF16)
            out_ref[song] = lax.dot_general(
                x, order, (((0,), (0,)), ((), ())), preferred_element_type=F32
            ).astype(BF16)
    code_wait(SEQ - 1, csend_sem)

    @pl.when(jnp.logical_or(to_next, to_prev))
    def _():
        code_wait(SEQ, csend_sem)


def body(
    bottom_codes, cond_codes, bottom_table, cond_table, conv_dilated, conv_mix,
    projection, norm_gain, norm_bias, attn_weight,
):
    vmem = pl.BlockSpec(memory_space=pltpu.VMEM)
    hbm = pl.BlockSpec(memory_space=pl.ANY)
    dma = pltpu.SemaphoreType.DMA
    out = pl.pallas_call(
        kernel,
        out_shape=pltpu.VMEM((4, ATTN, ROWS), BF16),
        in_specs=[vmem] * 4 + [hbm] * 6,
        out_specs=vmem,
        scratch_shapes=[
            pltpu.VMEM((VOCAB * 8 + 8, 128), F32),
            pltpu.VMEM((VOCAB * 8, 128), F32),
            pltpu.VMEM((4, STAGE, CH), BF16),
            pltpu.VMEM((3 * CH, CH), BF16),
            pltpu.VMEM((CH, CH), BF16),
            pltpu.VMEM((CH, WIDTH), BF16),
            pltpu.VMEM((3 * ATTN, WIDTH), BF16),
            pltpu.VMEM((2, 8, 128), I32),
            pltpu.VMEM((SLOTS, 8, 128), I32),
            pltpu.VMEM((BLOCKS, 128), I32),
            pltpu.SMEM((BLOCKS, 128), I32),
            pltpu.VMEM((2, GROUPS * PITCH, 128), F32),
            pltpu.VMEM((2, GROUPS * PITCH, 128), F32),
            pltpu.VMEM((CHUNK, 3 * CH), BF16),
            pltpu.VMEM((CHUNK, CH), BF16),
            pltpu.VMEM((CHUNK, CH), BF16),
            pltpu.VMEM((CHUNK, WIDTH), F32),
            pltpu.VMEM((CHUNK, WIDTH), BF16),
            pltpu.VMEM((3, CHUNK, ATTN), BF16),
            pltpu.VMEM((4, 8 * CPITCH, 128), F32),
            pltpu.VMEM((CHUNKS, SEQ, 8, ATTN), BF16),
            pltpu.VMEM((4, SEQ // 2, 2, 8, ATTN), BF16),
            dma((4,)),
            dma((4,)),
            dma,
            dma((3,)),
            dma((2,)),
            dma((CHUNKS,)),
            dma((CHUNKS,)),
            dma((CHUNKS,)),
        ],
        compiler_params=pltpu.CompilerParams(
            collective_id=0, has_side_effects=True, vmem_limit_bytes=63 * 1024 * 1024
        ),
        cost_estimate=pl.CostEstimate(
            flops=18_300_000_000, bytes_accessed=28_000_000, transcendentals=300_000
        ),
        name="upsampler",
    )(
        bottom_codes, cond_codes, norm_gain.reshape(WIDTH // 128, 128),
        norm_bias.reshape(WIDTH // 128, 128),
        bottom_table, cond_table, conv_dilated.reshape(3 * CH, CH), conv_mix, projection,
        attn_weight.T,
    )
    return out.transpose(0, 2, 1)


def solution(mesh):
    split = P(None, ("ctx", "seq"))
    return jax.shard_map(
        body,
        mesh=mesh,
        in_specs=(split, split) + (P(),) * 8,
        out_specs=P(None, ("ctx", "seq"), None),
        check_vma=False,
    )
```

```python
import functools
import math

import jax
import jax.numpy as jnp
from jax import lax
from jax.experimental import pallas as pl
from jax.experimental.pallas import tpu as pltpu
from jax.sharding import PartitionSpec as P

F32, BF16, I32 = jnp.float32, jnp.bfloat16, jnp.int32
MESH = pl.DeviceIdType.MESH

BLOCK = 128
DIL_BLOCKS, DIL_REST = divmod(2187, BLOCK)
CTX, SEQ = 4, 32
ROWS = 256
HALO = 9
SLOTS = SEQ + 2 * HALO
BLOCKS = 64
COLS = 4
CHUNK = BLOCKS * COLS
HALF = CHUNK // 2
CHUNKS = 4
VOCAB, CH, WIDTH, ATTN = 2048, 1024, 1920, 480
GROUPS = CH // 128
PITCH = CHUNK + 8
CPITCH = SEQ + 8
NOWHERE = VOCAB * 8
STAGE = 512
OWN, LEFT, RIGHT = 0, 8, 16
COND = 32
TAPS = ((LEFT, (0, 0, 0, 1)), (OWN, (0, 0, 0, 0)), (RIGHT, (0, 1, 1, 1)))


def kernel(
    bottom_ref, cond_ref, gain_ref, bias_ref, btab, ctab, conv, mix, proj, attn,
    out_ref,
    tb, tc, stage, wconv, wmix, wproj, wattn,
    sendc, codes, gath, gsm,
    stream, act, lhs, hidden, resid, pj, normed, qkv, att, sendo, got,
    stage_sem, w_sem, csend_sem, crecv_sem, g_sem, osend_sem, orecv_sem, local_sem,
):
    a = lax.axis_index("ctx")
    j = lax.axis_index("seq")
    k = j // 2
    h = j % 2

    to_next = jnp.logical_and(a < CTX - 1, j >= SEQ - HALO)
    to_prev = jnp.logical_and(a > 0, j < HALO)

    barrier = pltpu.get_barrier_semaphore()

    def greet(t, _):
        pl.semaphore_signal(
            barrier, inc=1, device_id=(a, lax.rem(j + t, SEQ)), device_id_type=MESH
        )
        return 0

    lax.fori_loop(1, SEQ, greet, 0)

    @pl.when(a > 0)
    def _():
        def f(t, _):
            pl.semaphore_signal(barrier, inc=1, device_id=(a - 1, t), device_id_type=MESH)
            return 0

        lax.fori_loop(SEQ - HALO, SEQ, f, 0)

    @pl.when(a < CTX - 1)
    def _():
        def f(t, _):
            pl.semaphore_signal(barrier, inc=1, device_id=(a + 1, t), device_id_type=MESH)
            return 0

        lax.fori_loop(0, HALO, f, 0)

    def stage_copy(i):
        table = (btab, ctab)[i // 4]
        return pltpu.make_async_copy(
            table.at[pl.ds((i % 4) * STAGE, STAGE)], stage.at[i % 4], stage_sem.at[i % 4]
        )

    weights = [
        pltpu.make_async_copy(src, dst, w_sem.at[i])
        for i, (src, dst) in enumerate(
            ((conv, wconv), (mix, wmix), (proj, wproj), (attn, wattn))
        )
    ]
    for i in range(4):
        stage_copy(i).start()

    sendc[...] = jnp.zeros_like(sendc)
    for song in range(4):
        p, s = divmod(song, 2)
        for u in range(2):
            sendc[p, 2 * s + u : 2 * s + u + 1, :] = bottom_ref[
                song : song + 1, u * 128 : (u + 1) * 128
            ]
            sendc[p, 4 + s : 5 + s, u * 64 : (u + 1) * 64] = cond_ref[song : song + 1, :]

    def widen(i):
        table = (tb, tc)[i // 4]
        stage_copy(i).wait()

        def f(r, _):
            x = stage[i % 4, pl.ds(r * 16, 16), :].astype(F32)
            base = ((i % 4) * STAGE + r * 16) * 8
            for q in range(2):
                for g in range(GROUPS):
                    table[pl.ds(base + q * 64 + g, 8, stride=8), :] = x[
                        8 * q : 8 * q + 8, 128 * g : 128 * g + 128
                    ]
            return 0

        lax.fori_loop(0, STAGE // 16, f, 0, unroll=2)
        if i + 4 < 8:
            stage_copy(i + 4).start()

    for i in range(2):
        widen(i)

    pl.semaphore_wait(barrier, SEQ - 1 + jnp.where(jnp.logical_or(to_next, to_prev), SEQ, 0))

    def send_codes(ctx, peer, slot, sem):
        pltpu.make_async_remote_copy(
            src_ref=sendc.at[peer % 2],
            dst_ref=codes.at[slot],
            send_sem=csend_sem,
            recv_sem=crecv_sem.at[sem],
            device_id=(ctx, peer),
            device_id_type=MESH,
        ).start()

    def own_codes(t, _):
        send_codes(a, lax.rem(j + t, SEQ), j + HALO, 0)
        return 0

    lax.fori_loop(1, SEQ, own_codes, 0)

    @pl.when(to_next)
    def _():
        def f(t, _):
            send_codes(a + 1, t, j - (SEQ - HALO), 1)
            return 0

        lax.fori_loop(0, SEQ, f, 0)

    @pl.when(to_prev)
    def _():
        def f(t, _):
            send_codes(a - 1, t, j + SEQ + HALO, 2)
            return 0

        lax.fori_loop(0, SEQ, f, 0)

    codes[j + HALO] = sendc[h]
    outside = jnp.where(lax.broadcasted_iota(I32, (HALO, 8, 128), 1) < 4, VOCAB, 0)

    @pl.when(a == 0)
    def _():
        codes[0:HALO] = outside

    @pl.when(a == CTX - 1)
    def _():
        codes[SEQ + HALO : SLOTS] = outside

    for i in range(2, 4):
        widen(i)
    for w in weights:
        w.start()
    tb[pl.ds(NOWHERE, 8), :] = jnp.full((8, 128), -1e9, F32)

    for i in range(4, 8):
        widen(i)

    def code_wait(count, sem):
        view = codes.at[pl.ds(0, count)]
        pltpu.make_async_copy(view, view, sem).wait()

    code_wait(SEQ - 1, crecv_sem.at[0])

    @pl.when(a > 0)
    def _():
        code_wait(HALO, crecv_sem.at[1])

    @pl.when(a < CTX - 1)
    def _():
        code_wait(HALO, crecv_sem.at[2])

    lanes = lax.broadcasted_iota(I32, (BLOCKS // 2, 128), 1)

    def to_smem(s):
        rows = pl.ds(s * SEQ, SEQ)
        return pltpu.make_async_copy(gath.at[rows], gsm.at[rows], g_sem.at[s])

    for s in range(2):
        pair = None
        for v in range(2):
            def bottom(beta):
                d, u = divmod(beta, 2)
                return codes[d : d + BLOCKS // 2, 2 * s + u, :]

            def upper(beta):
                d, u = divmod(beta, 2)
                x = codes[d : d + BLOCKS // 2, 4 + s, :]
                if u:
                    y = codes[d + 1 : d + 1 + BLOCKS // 2, 4 + s, :]
                    x = jnp.where(lanes < 64, x, y)
                return x, 32 * u

            lead = v + 2 * HALO
            before, after = lead - DIL_BLOCKS, lead + DIL_BLOCKS
            left = jnp.where(lanes >= 128 - DIL_REST, bottom(before - 1), bottom(before))
            right = jnp.where(lanes < DIL_REST, bottom(after + 1), bottom(after))
            up_own, own0 = upper(lead)
            up_left, left0 = upper(before - 1)
            up_right, right0 = upper(after)
            row = None
            for x, lane0, first, step in (
                (bottom(lead), OWN, 0, 8),
                (left, LEFT, -DIL_REST, 8),
                (right, RIGHT, DIL_REST, 8),
                (up_own, COND + OWN, own0, 2),
                (up_left, COND + LEFT, left0 + 32 - 3, 2),
                (up_right, COND + RIGHT, right0 + 2, 2),
            ):
                lane0 += 64 * v
                amount = lax.rem(lane0 - first + 256 - step * k, 128)
                rolled = pltpu.roll(x, amount, 1)
                row = rolled if row is None else jnp.where(lanes >= lane0, rolled, row)
            pair = row if pair is None else jnp.where(lanes < 64, pair, row)
        gath[s * SEQ : (s + 1) * SEQ, :] = pair * 8
        to_smem(s).start()
    to_smem(0).wait()

    scale = 1.0 / math.sqrt(ATTN)
    ri = lax.broadcasted_iota(I32, (CHUNK, CHUNK), 0)
    ci = lax.broadcasted_iota(I32, (CHUNK, CHUNK), 1)
    allowed = jnp.logical_and(
        (ri // SEQ) % COLS == (ci // SEQ) % COLS,
        2 * (ci % SEQ) + ci // HALF <= 2 * (ri % SEQ) + ri // HALF,
    )

    def gather_rows(i, first, count):
        s, p = divmod(i, 2)
        for q in range(count):
            b = first + q
            r, at = s * SEQ + b // 2, (q % 2) * 64
            row = b // 2 + (q % 2) * HALF
            for t, (lane0, conds) in enumerate(TAPS):
                upper = [
                    tc[pl.ds(gsm[r, at + COND + lane0 + p + c], 8), :]
                    for c in range(max(conds) + 1)
                ]
                for c in range(COLS):
                    x = tb[pl.ds(gsm[r, at + lane0 + COLS * p + c], 8), :] + upper[conds[c]]
                    if t == 1:
                        stream[i % 2, pl.ds(row + c * SEQ, 8, stride=PITCH), :] = x
                    else:
                        act[t // 2, pl.ds(row + c * SEQ, 8, stride=PITCH), :] = x

    def pack_rows(i, first, count):
        for t in range(3):
            for g in range(GROUPS):
                rows = pl.ds(g * PITCH + first, count)
                x = stream[i % 2, rows, :] if t == 1 else act[t // 2, rows, :]
                lhs[first : first + count, t * CH + g * 128 : t * CH + (g + 1) * 128] = (
                    jnp.maximum(x, 0.0).astype(BF16)
                )

    def convolve(i, n):
        cols = slice(n * 256, (n + 1) * 256)
        acc = jnp.dot(lhs[...], wconv[:, cols], preferred_element_type=F32)
        hidden[:, cols] = jnp.maximum(acc, 0.0).astype(BF16)

    def mix_rows(i):
        for n in range(CH // 256):
            acc = jnp.dot(
                hidden[...], wmix[:, n * 256 : (n + 1) * 256], preferred_element_type=F32
            )
            for g in range(2):
                own = stream[i % 2, pl.ds((2 * n + g) * PITCH, CHUNK), :]
                resid[:, n * 256 + g * 128 : n * 256 + (g + 1) * 128] = (
                    own + acc[:, g * 128 : (g + 1) * 128]
                ).astype(BF16)

    def project(n0, n1):
        pj[:, n0:n1] = jnp.dot(resid[...], wproj[:, n0:n1], preferred_element_type=F32)

    def normalise(first, count):
        rows = slice(first, first + count)
        x = pj[rows, :]
        x = x - jnp.mean(x, axis=-1, keepdims=True)
        var = jnp.mean(x * x, axis=-1, keepdims=True)
        x = x * lax.rsqrt(var + 1e-05)
        for g in range(WIDTH // 128):
            y = x[:, g * 128 : (g + 1) * 128] * gain_ref[g : g + 1, :] + bias_ref[g : g + 1, :]
            normed[rows, g * 128 : (g + 1) * 128] = y.astype(BF16)

    def make_qkv(n):
        qkv[n] = lax.dot_general(
            normed[...],
            wattn[n * ATTN : (n + 1) * ATTN, :],
            (((1,), (1,)), ((), ())),
            preferred_element_type=F32,
        ).astype(BF16)

    def attend():
        scores = lax.dot_general(
            qkv[0], qkv[1], (((1,), (1,)), ((), ())), preferred_element_type=F32
        ) * scale
        scores = jnp.where(allowed, scores, -jnp.inf)
        e = jnp.exp(scores - jnp.max(scores, axis=-1, keepdims=True))
        w = (e * (1.0 / jnp.sum(e, axis=-1, keepdims=True))).astype(BF16)
        mixed = jnp.dot(w, qkv[2], preferred_element_type=F32)
        for g in range(4):
            wide = min(128, ATTN - g * 128)
            for c in range(8):
                att[g, c * CPITCH : c * CPITCH + SEQ, 0:wide] = mixed[
                    c * SEQ : (c + 1) * SEQ, g * 128 : g * 128 + wide
                ]

    def regroup_rows(i):
        def regroup(d, _):
            for g in range(4):
                x = att[g, pl.ds(d, 8, stride=CPITCH), :]
                wide = min(128, ATTN - g * 128)
                sendo[i, d, :, g * 128 : g * 128 + wide] = x[:, :wide].astype(BF16)
            return 0

        lax.fori_loop(0, SEQ, regroup, 0, unroll=True)

    def send_rows(i):
        s, p = divmod(i, 2)
        song = 2 * h + s

        def send_out(t, _):
            peer = lax.rem(j + t, SEQ)
            pltpu.make_async_remote_copy(
                src_ref=sendo.at[i, peer],
                dst_ref=got.at[song, k, p],
                send_sem=osend_sem.at[i],
                recv_sem=orecv_sem.at[i],
                device_id=(a, peer),
                device_id_type=MESH,
            ).start()
            return 0

        lax.fori_loop(1, SEQ, send_out, 0, unroll=True)
        pltpu.make_async_copy(sendo.at[i, j], got.at[song, k, p], local_sem.at[i]).start()

    def first_rows(e, _):
        gather_rows(0, e * 8, 8)
        return 0

    lax.fori_loop(0, BLOCKS // 8, first_rows, 0)
    for q in range(4):
        pack_rows(0, q * 64, 64)

    for i in range(CHUNKS):
        if i == 0:
            weights[0].wait()

        for n in range(CH // 256):
            convolve(i, n)
            if i + 1 < CHUNKS:
                gather_rows(i + 1, n * 16, 16)
        if i == 0:
            weights[1].wait()
        mix_rows(i)
        if i == 0:
            weights[2].wait()
        for q, (n0, n1) in enumerate(((0, 512), (512, 1024), (1024, 1536), (1536, WIDTH))):
            project(n0, n1)
            if i + 1 < CHUNKS:
                pack_rows(i + 1, q * 64, 64)
        normalise(0, CHUNK)
        if i == 0:
            weights[3].wait()
            to_smem(1).wait()
        for n in range(3):
            make_qkv(n)
        attend()
        regroup_rows(i)
        send_rows(i)

    ri = lax.broadcasted_iota(I32, (ROWS, ROWS), 0)
    ci = lax.broadcasted_iota(I32, (ROWS, ROWS), 1)
    place = (ri // 8) * COLS + ri % COLS + ((ri // COLS) % 2) * BLOCK
    order = jnp.where(place == ci, 1.0, 0.0).astype(BF16)
    for s in range(2):
        for i in (2 * s, 2 * s + 1):
            view = sendo.at[i, pl.ds(0, SEQ - 1)]
            pltpu.make_async_copy(view, view, osend_sem.at[i]).wait()
            pltpu.make_async_copy(view, view, orecv_sem.at[i]).wait()
            pltpu.make_async_copy(
                sendo.at[i, j], got.at[2 * h + s, k, i % 2], local_sem.at[i]
            ).wait()
        for song in (s, s + 2):
            x = got[song].astype(F32).reshape(ROWS, ATTN).astype(BF16)
            out_ref[song] = lax.dot_general(
                x, order, (((0,), (0,)), ((), ())), preferred_element_type=F32
            ).astype(BF16)
    code_wait(SEQ - 1, csend_sem)

    @pl.when(jnp.logical_or(to_next, to_prev))
    def _():
        code_wait(SEQ, csend_sem)


def body(
    bottom_codes, cond_codes, bottom_table, cond_table, conv_dilated, conv_mix,
    projection, norm_gain, norm_bias, attn_weight,
):
    vmem = pl.BlockSpec(memory_space=pltpu.VMEM)
    hbm = pl.BlockSpec(memory_space=pl.ANY)
    dma = pltpu.SemaphoreType.DMA
    out = pl.pallas_call(
        kernel,
        out_shape=pltpu.VMEM((4, ATTN, ROWS), BF16),
        in_specs=[vmem] * 4 + [hbm] * 6,
        out_specs=vmem,
        scratch_shapes=[
            pltpu.VMEM((VOCAB * 8 + 8, 128), F32),
            pltpu.VMEM((VOCAB * 8, 128), F32),
            pltpu.VMEM((4, STAGE, CH), BF16),
            pltpu.VMEM((3 * CH, CH), BF16),
            pltpu.VMEM((CH, CH), BF16),
            pltpu.VMEM((CH, WIDTH), BF16),
            pltpu.VMEM((3 * ATTN, WIDTH), BF16),
            pltpu.VMEM((2, 8, 128), I32),
            pltpu.VMEM((SLOTS, 8, 128), I32),
            pltpu.VMEM((BLOCKS, 128), I32),
            pltpu.SMEM((BLOCKS, 128), I32),
            pltpu.VMEM((2, GROUPS * PITCH, 128), F32),
            pltpu.VMEM((2, GROUPS * PITCH, 128), F32),
            pltpu.VMEM((CHUNK, 3 * CH), BF16),
            pltpu.VMEM((CHUNK, CH), BF16),
            pltpu.VMEM((CHUNK, CH), BF16),
            pltpu.VMEM((CHUNK, WIDTH), F32),
            pltpu.VMEM((CHUNK, WIDTH), BF16),
            pltpu.VMEM((3, CHUNK, ATTN), BF16),
            pltpu.VMEM((4, 8 * CPITCH, 128), F32),
            pltpu.VMEM((CHUNKS, SEQ, 8, ATTN), BF16),
            pltpu.VMEM((4, SEQ // 2, 2, 8, ATTN), BF16),
            dma((4,)),
            dma((4,)),
            dma,
            dma((3,)),
            dma((2,)),
            dma((CHUNKS,)),
            dma((CHUNKS,)),
            dma((CHUNKS,)),
        ],
        compiler_params=pltpu.CompilerParams(
            collective_id=0, has_side_effects=True, vmem_limit_bytes=63 * 1024 * 1024
        ),
        cost_estimate=pl.CostEstimate(
            flops=18_300_000_000, bytes_accessed=28_000_000, transcendentals=300_000
        ),
        name="upsampler",
    )(
        bottom_codes, cond_codes, norm_gain.reshape(WIDTH // 128, 128),
        norm_bias.reshape(WIDTH // 128, 128),
        bottom_table, cond_table, conv_dilated.reshape(3 * CH, CH), conv_mix, projection,
        attn_weight.T,
    )
    return out.transpose(0, 2, 1)


def solution(mesh):
    split = P(None, ("ctx", "seq"))
    return jax.shard_map(
        body,
        mesh=mesh,
        in_specs=(split, split) + (P(),) * 8,
        out_specs=P(None, ("ctx", "seq"), None),
        check_vma=False,
    )
```

```python
import functools
import math

import jax
import jax.numpy as jnp
from jax import lax
from jax.experimental import pallas as pl
from jax.experimental.pallas import tpu as pltpu
from jax.sharding import PartitionSpec as P

F32, BF16, I32 = jnp.float32, jnp.bfloat16, jnp.int32
MESH = pl.DeviceIdType.MESH

BLOCK = 128
DIL_BLOCKS, DIL_REST = divmod(2187, BLOCK)
CTX, SEQ = 4, 32
ROWS = 256
HALO = 9
SLOTS = SEQ + 2 * HALO
BLOCKS = 64
COLS = 4
CHUNK = BLOCKS * COLS
HALF = CHUNK // 2
CHUNKS = 4
VOCAB, CH, WIDTH, ATTN = 2048, 1024, 1920, 480
GROUPS = CH // 128
PITCH = CHUNK + 8
CPITCH = SEQ + 8
NOWHERE = VOCAB * 8
STAGE = 512
OWN, LEFT, RIGHT = 0, 8, 16
COND = 32
TAPS = ((LEFT, (0, 0, 0, 1)), (OWN, (0, 0, 0, 0)), (RIGHT, (0, 1, 1, 1)))


def kernel(
    bottom_ref, cond_ref, gain_ref, bias_ref, btab, ctab, conv, mix, proj, attn,
    out_ref,
    tb, tc, stage, wconv, wmix, wproj, wattn,
    sendc, codes, gath, gsm,
    stream, act, lhs, hidden, resid, pj, normed, qkv, att, sendo, got,
    stage_sem, w_sem, csend_sem, crecv_sem, g_sem, osend_sem, orecv_sem, local_sem,
):
    a = lax.axis_index("ctx")
    j = lax.axis_index("seq")
    k = j // 2
    h = j % 2

    to_next = jnp.logical_and(a < CTX - 1, j >= SEQ - HALO)
    to_prev = jnp.logical_and(a > 0, j < HALO)

    barrier = pltpu.get_barrier_semaphore()

    def greet(t, _):
        pl.semaphore_signal(
            barrier, inc=1, device_id=(a, lax.rem(j + t, SEQ)), device_id_type=MESH
        )
        return 0

    lax.fori_loop(1, SEQ, greet, 0)

    @pl.when(a > 0)
    def _():
        def f(t, _):
            pl.semaphore_signal(barrier, inc=1, device_id=(a - 1, t), device_id_type=MESH)
            return 0

        lax.fori_loop(SEQ - HALO, SEQ, f, 0)

    @pl.when(a < CTX - 1)
    def _():
        def f(t, _):
            pl.semaphore_signal(barrier, inc=1, device_id=(a + 1, t), device_id_type=MESH)
            return 0

        lax.fori_loop(0, HALO, f, 0)

    def stage_copy(i):
        table = (btab, ctab)[i // 4]
        return pltpu.make_async_copy(
            table.at[pl.ds((i % 4) * STAGE, STAGE)], stage.at[i % 4], stage_sem.at[i % 4]
        )

    weights = [
        pltpu.make_async_copy(src, dst, w_sem.at[i])
        for i, (src, dst) in enumerate(
            ((conv, wconv), (mix, wmix), (proj, wproj), (attn, wattn))
        )
    ]
    for i in range(4):
        stage_copy(i).start()

    sendc[...] = jnp.zeros_like(sendc)
    for song in range(4):
        p, s = divmod(song, 2)
        for u in range(2):
            sendc[p, 2 * s + u : 2 * s + u + 1, :] = bottom_ref[
                song : song + 1, u * 128 : (u + 1) * 128
            ]
            sendc[p, 4 + s : 5 + s, u * 64 : (u + 1) * 64] = cond_ref[song : song + 1, :]

    def widen(i):
        table = (tb, tc)[i // 4]
        stage_copy(i).wait()

        def f(r, _):
            x = stage[i % 4, pl.ds(r * 16, 16), :].astype(F32)
            base = ((i % 4) * STAGE + r * 16) * 8
            for q in range(2):
                for g in range(GROUPS):
                    table[pl.ds(base + q * 64 + g, 8, stride=8), :] = x[
                        8 * q : 8 * q + 8, 128 * g : 128 * g + 128
                    ]
            return 0

        lax.fori_loop(0, STAGE // 16, f, 0, unroll=2)
        if i + 4 < 8:
            stage_copy(i + 4).start()

    for i in range(2):
        widen(i)

    pl.semaphore_wait(barrier, SEQ - 1 + jnp.where(jnp.logical_or(to_next, to_prev), SEQ, 0))

    def send_codes(ctx, peer, slot, sem):
        pltpu.make_async_remote_copy(
            src_ref=sendc.at[peer % 2],
            dst_ref=codes.at[slot],
            send_sem=csend_sem,
            recv_sem=crecv_sem.at[sem],
            device_id=(ctx, peer),
            device_id_type=MESH,
        ).start()

    def own_codes(t, _):
        send_codes(a, lax.rem(j + t, SEQ), j + HALO, 0)
        return 0

    lax.fori_loop(1, SEQ, own_codes, 0)

    @pl.when(to_next)
    def _():
        def f(t, _):
            send_codes(a + 1, t, j - (SEQ - HALO), 1)
            return 0

        lax.fori_loop(0, SEQ, f, 0)

    @pl.when(to_prev)
    def _():
        def f(t, _):
            send_codes(a - 1, t, j + SEQ + HALO, 2)
            return 0

        lax.fori_loop(0, SEQ, f, 0)

    codes[j + HALO] = sendc[h]
    outside = jnp.where(lax.broadcasted_iota(I32, (HALO, 8, 128), 1) < 4, VOCAB, 0)

    @pl.when(a == 0)
    def _():
        codes[0:HALO] = outside

    @pl.when(a == CTX - 1)
    def _():
        codes[SEQ + HALO : SLOTS] = outside

    for i in range(2, 4):
        widen(i)
    for w in weights:
        w.start()
    tb[pl.ds(NOWHERE, 8), :] = jnp.full((8, 128), -1e9, F32)

    for i in range(4, 8):
        widen(i)

    def code_wait(count, sem):
        view = codes.at[pl.ds(0, count)]
        pltpu.make_async_copy(view, view, sem).wait()

    code_wait(SEQ - 1, crecv_sem.at[0])

    @pl.when(a > 0)
    def _():
        code_wait(HALO, crecv_sem.at[1])

    @pl.when(a < CTX - 1)
    def _():
        code_wait(HALO, crecv_sem.at[2])

    lanes = lax.broadcasted_iota(I32, (BLOCKS // 2, 128), 1)

    def to_smem(s):
        rows = pl.ds(s * SEQ, SEQ)
        return pltpu.make_async_copy(gath.at[rows], gsm.at[rows], g_sem.at[s])

    for s in range(2):
        pair = None
        for v in range(2):
            def bottom(beta):
                d, u = divmod(beta, 2)
                return codes[d : d + BLOCKS // 2, 2 * s + u, :]

            def upper(beta):
                d, u = divmod(beta, 2)
                x = codes[d : d + BLOCKS // 2, 4 + s, :]
                if u:
                    y = codes[d + 1 : d + 1 + BLOCKS // 2, 4 + s, :]
                    x = jnp.where(lanes < 64, x, y)
                return x, 32 * u

            lead = v + 2 * HALO
            before, after = lead - DIL_BLOCKS, lead + DIL_BLOCKS
            left = jnp.where(lanes >= 128 - DIL_REST, bottom(before - 1), bottom(before))
            right = jnp.where(lanes < DIL_REST, bottom(after + 1), bottom(after))
            up_own, own0 = upper(lead)
            up_left, left0 = upper(before - 1)
            up_right, right0 = upper(after)
            row = None
            for x, lane0, first, step in (
                (bottom(lead), OWN, 0, 8),
                (left, LEFT, -DIL_REST, 8),
                (right, RIGHT, DIL_REST, 8),
                (up_own, COND + OWN, own0, 2),
                (up_left, COND + LEFT, left0 + 32 - 3, 2),
                (up_right, COND + RIGHT, right0 + 2, 2),
            ):
                lane0 += 64 * v
                amount = lax.rem(lane0 - first + 256 - step * k, 128)
                rolled = pltpu.roll(x, amount, 1)
                row = rolled if row is None else jnp.where(lanes >= lane0, rolled, row)
            pair = row if pair is None else jnp.where(lanes < 64, pair, row)
        gath[s * SEQ : (s + 1) * SEQ, :] = pair * 8
        to_smem(s).start()
    to_smem(0).wait()

    scale = 1.0 / math.sqrt(ATTN)
    ri = lax.broadcasted_iota(I32, (CHUNK, CHUNK), 0)
    ci = lax.broadcasted_iota(I32, (CHUNK, CHUNK), 1)
    allowed = jnp.logical_and(
        (ri // SEQ) % COLS == (ci // SEQ) % COLS,
        2 * (ci % SEQ) + ci // HALF <= 2 * (ri % SEQ) + ri // HALF,
    )

    def gather_rows(i, first, count):
        s, p = divmod(i, 2)
        for q in range(count):
            b = first + q
            r, at = s * SEQ + b // 2, (q % 2) * 64
            row = b // 2 + (q % 2) * HALF
            for t, (lane0, conds) in enumerate(TAPS):
                upper = [
                    tc[pl.ds(gsm[r, at + COND + lane0 + p + c], 8), :]
                    for c in range(max(conds) + 1)
                ]
                for c in range(COLS):
                    x = tb[pl.ds(gsm[r, at + lane0 + COLS * p + c], 8), :] + upper[conds[c]]
                    if t == 1:
                        stream[i % 2, pl.ds(row + c * SEQ, 8, stride=PITCH), :] = x
                    else:
                        act[t // 2, pl.ds(row + c * SEQ, 8, stride=PITCH), :] = x

    def pack_rows(i, first, count):
        for t in range(3):
            for g in range(GROUPS):
                rows = pl.ds(g * PITCH + first, count)
                x = stream[i % 2, rows, :] if t == 1 else act[t // 2, rows, :]
                lhs[first : first + count, t * CH + g * 128 : t * CH + (g + 1) * 128] = (
                    jnp.maximum(x, 0.0).astype(BF16)
                )

    def convolve(i, n):
        cols = slice(n * 256, (n + 1) * 256)
        acc = jnp.dot(lhs[...], wconv[:, cols], preferred_element_type=F32)
        hidden[:, cols] = jnp.maximum(acc, 0.0).astype(BF16)

    def mix_rows(i):
        for n in range(CH // 256):
            acc = jnp.dot(
                hidden[...], wmix[:, n * 256 : (n + 1) * 256], preferred_element_type=F32
            )
            for g in range(2):
                own = stream[i % 2, pl.ds((2 * n + g) * PITCH, CHUNK), :]
                resid[:, n * 256 + g * 128 : n * 256 + (g + 1) * 128] = (
                    own + acc[:, g * 128 : (g + 1) * 128]
                ).astype(BF16)

    def project(n0, n1):
        pj[:, n0:n1] = jnp.dot(resid[...], wproj[:, n0:n1], preferred_element_type=F32)

    def normalise(first, count):
        rows = slice(first, first + count)
        x = pj[rows, :]
        x = x - jnp.mean(x, axis=-1, keepdims=True)
        var = jnp.mean(x * x, axis=-1, keepdims=True)
        x = x * lax.rsqrt(var + 1e-05)
        for g in range(WIDTH // 128):
            y = x[:, g * 128 : (g + 1) * 128] * gain_ref[g : g + 1, :] + bias_ref[g : g + 1, :]
            normed[rows, g * 128 : (g + 1) * 128] = y.astype(BF16)

    def make_qkv(n):
        qkv[n] = lax.dot_general(
            normed[...],
            wattn[n * ATTN : (n + 1) * ATTN, :],
            (((1,), (1,)), ((), ())),
            preferred_element_type=F32,
        ).astype(BF16)

    def attend():
        scores = lax.dot_general(
            qkv[0], qkv[1], (((1,), (1,)), ((), ())), preferred_element_type=F32
        ) * scale
        scores = jnp.where(allowed, scores, -jnp.inf)
        e = jnp.exp(scores - jnp.max(scores, axis=-1, keepdims=True))
        w = (e * (1.0 / jnp.sum(e, axis=-1, keepdims=True))).astype(BF16)
        mixed = jnp.dot(w, qkv[2], preferred_element_type=F32)
        for g in range(4):
            wide = min(128, ATTN - g * 128)
            for c in range(8):
                att[g, c * CPITCH : c * CPITCH + SEQ, 0:wide] = mixed[
                    c * SEQ : (c + 1) * SEQ, g * 128 : g * 128 + wide
                ]

    def regroup_rows(i):
        def regroup(d, _):
            for g in range(4):
                x = att[g, pl.ds(d, 8, stride=CPITCH), :]
                wide = min(128, ATTN - g * 128)
                sendo[i, d, :, g * 128 : g * 128 + wide] = x[:, :wide].astype(BF16)
            return 0

        lax.fori_loop(0, SEQ, regroup, 0, unroll=True)

    def send_rows(i):
        s, p = divmod(i, 2)
        song = 2 * h + s

        def send_out(t, _):
            peer = lax.rem(j + t, SEQ)
            pltpu.make_async_remote_copy(
                src_ref=sendo.at[i, peer],
                dst_ref=got.at[song, k, p],
                send_sem=osend_sem.at[i],
                recv_sem=orecv_sem.at[i],
                device_id=(a, peer),
                device_id_type=MESH,
            ).start()
            return 0

        lax.fori_loop(1, SEQ, send_out, 0, unroll=True)
        pltpu.make_async_copy(sendo.at[i, j], got.at[song, k, p], local_sem.at[i]).start()

    def first_rows(e, _):
        gather_rows(0, e * 16, 16)
        return 0

    lax.fori_loop(0, BLOCKS // 16, first_rows, 0)
    for q in range(4):
        pack_rows(0, q * 64, 64)

    for i in range(CHUNKS):
        if i == 0:
            weights[0].wait()

        for n in range(CH // 256):
            convolve(i, n)
            if i + 1 < CHUNKS:
                gather_rows(i + 1, n * 16, 16)
        if i == 0:
            weights[1].wait()
        mix_rows(i)
        if i == 0:
            weights[2].wait()
        for q, (n0, n1) in enumerate(((0, 512), (512, 1024), (1024, 1536), (1536, WIDTH))):
            project(n0, n1)
            if i + 1 < CHUNKS:
                pack_rows(i + 1, q * 64, 64)
        normalise(0, CHUNK)
        if i == 0:
            weights[3].wait()
            to_smem(1).wait()
        for n in range(3):
            make_qkv(n)
        attend()
        regroup_rows(i)
        send_rows(i)

    ri = lax.broadcasted_iota(I32, (ROWS, ROWS), 0)
    ci = lax.broadcasted_iota(I32, (ROWS, ROWS), 1)
    place = (ri // 8) * COLS + ri % COLS + ((ri // COLS) % 2) * BLOCK
    order = jnp.where(place == ci, 1.0, 0.0).astype(BF16)
    for s in range(2):
        for i in (2 * s, 2 * s + 1):
            view = sendo.at[i, pl.ds(0, SEQ - 1)]
            pltpu.make_async_copy(view, view, osend_sem.at[i]).wait()
            pltpu.make_async_copy(view, view, orecv_sem.at[i]).wait()
            pltpu.make_async_copy(
                sendo.at[i, j], got.at[2 * h + s, k, i % 2], local_sem.at[i]
            ).wait()
        for song in (s, s + 2):
            x = got[song].astype(F32).reshape(ROWS, ATTN).astype(BF16)
            out_ref[song] = lax.dot_general(
                x, order, (((0,), (0,)), ((), ())), preferred_element_type=F32
            ).astype(BF16)
    code_wait(SEQ - 1, csend_sem)

    @pl.when(jnp.logical_or(to_next, to_prev))
    def _():
        code_wait(SEQ, csend_sem)


def body(
    bottom_codes, cond_codes, bottom_table, cond_table, conv_dilated, conv_mix,
    projection, norm_gain, norm_bias, attn_weight,
):
    vmem = pl.BlockSpec(memory_space=pltpu.VMEM)
    hbm = pl.BlockSpec(memory_space=pl.ANY)
    dma = pltpu.SemaphoreType.DMA
    out = pl.pallas_call(
        kernel,
        out_shape=pltpu.VMEM((4, ATTN, ROWS), BF16),
        in_specs=[vmem] * 4 + [hbm] * 6,
        out_specs=vmem,
        scratch_shapes=[
            pltpu.VMEM((VOCAB * 8 + 8, 128), F32),
            pltpu.VMEM((VOCAB * 8, 128), F32),
            pltpu.VMEM((4, STAGE, CH), BF16),
            pltpu.VMEM((3 * CH, CH), BF16),
            pltpu.VMEM((CH, CH), BF16),
            pltpu.VMEM((CH, WIDTH), BF16),
            pltpu.VMEM((3 * ATTN, WIDTH), BF16),
            pltpu.VMEM((2, 8, 128), I32),
            pltpu.VMEM((SLOTS, 8, 128), I32),
            pltpu.VMEM((BLOCKS, 128), I32),
            pltpu.SMEM((BLOCKS, 128), I32),
            pltpu.VMEM((2, GROUPS * PITCH, 128), F32),
            pltpu.VMEM((2, GROUPS * PITCH, 128), F32),
            pltpu.VMEM((CHUNK, 3 * CH), BF16),
            pltpu.VMEM((CHUNK, CH), BF16),
            pltpu.VMEM((CHUNK, CH), BF16),
            pltpu.VMEM((CHUNK, WIDTH), F32),
            pltpu.VMEM((CHUNK, WIDTH), BF16),
            pltpu.VMEM((3, CHUNK, ATTN), BF16),
            pltpu.VMEM((4, 8 * CPITCH, 128), F32),
            pltpu.VMEM((CHUNKS, SEQ, 8, ATTN), BF16),
            pltpu.VMEM((4, SEQ // 2, 2, 8, ATTN), BF16),
            dma((4,)),
            dma((4,)),
            dma,
            dma((3,)),
            dma((2,)),
            dma((CHUNKS,)),
            dma((CHUNKS,)),
            dma((CHUNKS,)),
        ],
        compiler_params=pltpu.CompilerParams(
            collective_id=0, has_side_effects=True, vmem_limit_bytes=63 * 1024 * 1024
        ),
        cost_estimate=pl.CostEstimate(
            flops=18_300_000_000, bytes_accessed=28_000_000, transcendentals=300_000
        ),
        name="upsampler",
    )(
        bottom_codes, cond_codes, norm_gain.reshape(WIDTH // 128, 128),
        norm_bias.reshape(WIDTH // 128, 128),
        bottom_table, cond_table, conv_dilated.reshape(3 * CH, CH), conv_mix, projection,
        attn_weight.T,
    )
    return out.transpose(0, 2, 1)


def solution(mesh):
    split = P(None, ("ctx", "seq"))
    return jax.shard_map(
        body,
        mesh=mesh,
        in_specs=(split, split) + (P(),) * 8,
        out_specs=P(None, ("ctx", "seq"), None),
        check_vma=False,
    )
```
